512 devices in a mesh: row: 32 (over x, y, core), tensor: 16 (over z).
Axes of the slice: x: 4, y: 4, z: 16, core: 2. Of those that a mesh axis runs over, the one named last changes fastest.
Arguments:
- ssm_input: bfloat16 [128, 8, 8192], P('row', None, 'tensor'), may hold values from -12 to 12
- gate_input: bfloat16 [128, 8, 8192], P('row', None, 'tensor'), may hold values from -6 to 6
- write_vectors: bfloat16 [128, 8, 4096], P('row', None, 'tensor'), may hold values from -0.375 to 0.375
- read_vectors: bfloat16 [128, 8, 4096], P('row', None, 'tensor'), may hold values from -6 to 6
- step_logit: float32 [128, 8, 128], P('row', None, 'tensor'), may hold values from -4 to 4
- step_bias: float32 [128], P('tensor'), may hold values from -2 to 0.5
- decay_rate: float32 [128], P('tensor'), may hold values from 0.05 to 4
- skip_gain: float32 [128], P('tensor'), may hold values from 0.5 to 1.5
- norm_gain: float32 [8192], P('tensor'), may hold values from 0.1 to 1.9
- ssm_state: bfloat16 [128, 128, 64, 256], P('row', 'tensor'), may hold values from -0.375 to 0.375
- accepted: int32 [128], P('row'), may hold values from 0 to 8
- out_weight: bfloat16 [8192, 8192], P('tensor', 'row'), may hold values from -0.0625 to 0.0625
- token_embeds: bfloat16 [128, 8, 8192], P('tensor', None, 'row'), may hold values from -6 to 6
- feat_weight: bfloat16 [8192, 8192], P('row', 'tensor'), may hold values from -0.0625 to 0.0625
- embed_weight: bfloat16 [8192, 8192], P('row', 'tensor'), may hold values from -0.0625 to 0.0625
Outputs:
- draft_hidden: bfloat16 [128, 8, 8192], P('row', None, 'tensor')
- new_state: bfloat16 [128, 128, 64, 256], P('row', 'tensor')
The draws below stay inside these ranges and needn't reach their ends.
All inputs are finite; a program needn't handle non-finite values.
Results may differ from the reference program's by a relative error of at most 0.0049.
Values may be sent and summed in bfloat16 or wider, within the bound.
A program may use at most 64 MiB of HBM per device.

```python
import math
import jax
import jax.numpy as jnp
from jax import lax

D = 8192
HEAD_DIM = 64
STATE = 256
HEADS_DEV = 8
DRAFT = 8
ROWS = 128
HEADS = 128
GROUPS = 16


def draw_ssm_input(key, part):
    key = jax.random.fold_in(key, 11)
    channels_all = HEADS * HEAD_DIM
    channel = jnp.arange(channels_all, dtype=jnp.float32) / (channels_all - 1)
    rising = 3.0 ** (0.5 * channel)
    sample_values = jnp.clip(jax.random.normal(key, (ROWS, DRAFT, channels_all), jnp.float32), -6.0, 6.0)
    return (sample_values * rising).astype(jnp.bfloat16)


def with_ends(entries, own_key, low, high):
    dims = entries.shape
    index_at = [jax.random.randint(jax.random.fold_in(own_key, axis), (), 0, dims[axis]) for axis in range(len(dims))]
    entries = entries.at[tuple(index_at)].set(low)
    longest = dims.index(max(dims))
    index_at[longest] = (index_at[longest] + 1) % dims[longest]
    return entries.at[tuple(index_at)].set(high)


def level_of(key, extent, cuts, smallest, high):
    def one(dim, blocks):
        heights = jax.random.uniform(jax.random.fold_in(jax.random.fold_in(key, 6), dim), (blocks,), jnp.float32, smallest / len(cuts), high / len(cuts))
        return jnp.repeat(jnp.exp(heights), extent[dim] // blocks).reshape((-1,) + (1,) * (len(extent) - dim - 1))

    gain = one(*cuts[0])
    for cut in cuts[1:]:
        gain = gain * one(*cut)
    return gain


def normal_values(own_key, shape, width, limit, shards=(), kind=jnp.bfloat16):
    factor_of = level_of(own_key, shape, shards, -0.22, 0.18) if shards else 1.0
    result = jax.random.normal(own_key, shape, jnp.float32) * width * factor_of
    return jnp.minimum(jnp.maximum(result, -limit), limit).astype(kind)


def setup_inputs(seed: int = 0) -> dict:
    arg_keys = jax.random.split(jax.random.key(seed), 16)
    ssm_input = draw_ssm_input(jax.random.fold_in(arg_keys[15], 71), 0)
    gate_input = normal_values(arg_keys[1], (ROWS, DRAFT, HEADS * HEAD_DIM), 1.0, 6.0, ((0, 32), (2, 16)))
    write_vectors = normal_values(arg_keys[2], (ROWS, DRAFT, GROUPS * STATE), 0.0625, 0.375, ((0, 32), (2, 16)))
    read_vectors = normal_values(arg_keys[3], (ROWS, DRAFT, GROUPS * STATE), 1.0, 6.0, ((0, 32), (2, 16)))
    step_logit = normal_values(arg_keys[4], (ROWS, DRAFT, HEADS), 1.0, 4.0, ((0, 32), (2, 16)), jnp.float32)
    step_bias = jnp.clip(-2.0 + 2.5 * jax.random.uniform(arg_keys[5], (HEADS,), jnp.float32) ** level_of(arg_keys[5], (HEADS,), ((0, 16),), -0.2, 0.2), -2.0, 0.5)
    decay_rate = jnp.clip(jnp.exp(math.log(4.0) - 4.3820266 * jax.random.uniform(arg_keys[6], (HEADS,), jnp.float32) ** level_of(arg_keys[6], (HEADS,), ((0, 16),), -0.2, 0.2)), 0.05, 4.0)
    skip_gain = jnp.clip(0.5 + 1.0 * jax.random.uniform(arg_keys[7], (HEADS,), jnp.float32) ** level_of(arg_keys[7], (HEADS,), ((0, 16),), -0.2, 0.2), 0.5, 1.5)
    norm_gain = jnp.clip(1.0 + 0.18 * jax.random.normal(arg_keys[8], (HEADS * HEAD_DIM,), jnp.float32), 0.1, 1.9)
    ssm_state = normal_values(arg_keys[9], (ROWS, HEADS, HEAD_DIM, STATE), 0.0625, 0.375, ((0, 32), (1, 16)))
    accepted = with_ends(jax.random.randint(arg_keys[10], (ROWS,), 0, DRAFT + 1), jax.random.fold_in(arg_keys[10], 1), 0, DRAFT).astype(jnp.int32)
    out_weight = normal_values(arg_keys[11], (HEADS * HEAD_DIM, D), (HEADS * HEAD_DIM) ** -0.5, 0.0625, ((0, 16), (1, 32)))
    token_embeds = normal_values(arg_keys[12], (ROWS, DRAFT, D), 1.0, 6.0, ((0, 16), (2, 32)))
    feat_weight = normal_values(arg_keys[13], (D, D), D ** -0.5, 0.0625, ((0, 32), (1, 16)))
    embed_weight = normal_values(arg_keys[14], (D, D), D ** -0.5, 0.0625, ((0, 32), (1, 16)))
    return {"ssm_input": ssm_input, "gate_input": gate_input, "write_vectors": write_vectors, "read_vectors": read_vectors, "step_logit": step_logit, "step_bias": step_bias, "decay_rate": decay_rate, "skip_gain": skip_gain, "norm_gain": norm_gain, "ssm_state": ssm_state, "accepted": accepted, "out_weight": out_weight, "token_embeds": token_embeds, "feat_weight": feat_weight, "embed_weight": embed_weight}


norm_eps = 1e-05

def row_mixer(ssm_row, gate_row, write_row, read_row, logit_row, state_row, accepted_row, step_bias, decay_rate, skip_gain, norm_gain):
    highest = lax.Precision.HIGHEST
    step_size = jax.nn.softplus(logit_row + step_bias[None, :])
    log_decay = jnp.cumsum(-step_size * decay_rate[None, :], axis=0)
    x_heads = ssm_row.astype(jnp.float32).reshape(DRAFT, HEADS, HEAD_DIM)
    write_heads = jnp.repeat(write_row.astype(jnp.float32).reshape(DRAFT, GROUPS, STATE), HEADS_DEV, axis=1)
    read_heads = jnp.repeat(read_row.astype(jnp.float32).reshape(DRAFT, GROUPS, STATE), HEADS_DEV, axis=1)
    intersection = jnp.einsum('thn,shn->tsh', read_heads, write_heads, precision=highest)
    positions = jnp.arange(DRAFT)
    lower = (positions[None, :] <= positions[:, None])[:, :, None]
    gap = log_decay[:, None, :] - log_decay[None, :, :]
    kernel_mix = jnp.where(lower, jnp.exp(jnp.where(lower, gap, 0.0)), 0.0) * intersection * step_size[None, :, :]
    intra = jnp.einsum('tsh,shp->thp', kernel_mix, x_heads, precision=highest)
    state_wide = state_row.astype(jnp.float32)
    carried = jnp.einsum('thn,hpn->thp', read_heads, state_wide, precision=highest)
    mixed = jnp.exp(log_decay)[:, :, None] * carried + intra + skip_gain[None, :, None] * x_heads
    gated = mixed.reshape(DRAFT, HEADS * HEAD_DIM) * jax.nn.silu(gate_row.astype(jnp.float32))
    mean_square = lax.optimization_barrier(jnp.mean(gated * gated, axis=-1, keepdims=True))
    normed = (gated * lax.rsqrt(mean_square + norm_eps) * norm_gain[None, :]).astype(jnp.bfloat16)
    padded_log = jnp.concatenate([jnp.zeros((1, HEADS), jnp.float32), log_decay], axis=0)
    chosen = (jnp.arange(DRAFT + 1) == accepted_row).astype(jnp.float32)
    end_log = jnp.dot(chosen, padded_log, precision=highest)
    kept = (positions < accepted_row)[:, None]
    weight_in = jnp.where(kept, jnp.exp(jnp.where(kept, end_log[None, :] - log_decay, 0.0)), 0.0) * step_size
    weighted_x = weight_in[:, :, None] * x_heads
    added = jnp.einsum('shp,shn->hpn', weighted_x, write_heads, precision=highest)
    new_row = (jnp.exp(end_log)[:, None, None] * state_wide + added).astype(jnp.bfloat16)
    return (normed, new_row)

def reference(ssm_input, gate_input, write_vectors, read_vectors, step_logit, step_bias, decay_rate, skip_gain, norm_gain, ssm_state, accepted, out_weight, token_embeds, feat_weight, embed_weight):

    def one_row(items):
        return row_mixer(items[0], items[1], items[2], items[3], items[4], items[5], items[6], step_bias, decay_rate, skip_gain, norm_gain)
    normed, new_state = lax.map(one_row, (ssm_input, gate_input, write_vectors, read_vectors, step_logit, ssm_state, accepted))
    normed_flat = normed.reshape(ROWS * DRAFT, HEADS * HEAD_DIM)
    feature = jnp.dot(normed_flat, out_weight, preferred_element_type=jnp.float32).astype(jnp.bfloat16)
    embeds_flat = token_embeds.reshape(ROWS * DRAFT, D)
    projected = jnp.dot(feature, feat_weight, preferred_element_type=jnp.float32) + jnp.dot(embeds_flat, embed_weight, preferred_element_type=jnp.float32)
    used = (jnp.arange(DRAFT)[None, :] <= accepted[:, None]).astype(jnp.float32)
    draft_hidden = (projected.reshape(ROWS, DRAFT, D) * used[:, :, None]).astype(jnp.bfloat16)
    return (draft_hidden, new_state)
```

```python
import functools

import jax
import jax.numpy as jnp
from jax import lax
from jax.experimental import pallas as pl
from jax.experimental.pallas import tpu as pltpu
from jax.sharding import PartitionSpec as P

norm_eps = 1e-05
MESH = pl.DeviceIdType.MESH
f32 = jnp.float32
bf16 = jnp.bfloat16


def nt_dot(a, b):
    return lax.dot_general(a, b, (((1,), (1,)), ((), ())), preferred_element_type=f32)


def split3(v):
    hi = v.astype(bf16).astype(f32)
    mid = (v - hi).astype(bf16).astype(f32)
    return hi, mid, v - hi - mid


def kernel(
    x_ref, gate_ref, b_ref, c_ref, logit_ref, bias_ref, decay_ref, skip_ref, gain_ref, acc_ref, emb_ref,
    state_hbm, wo_hbm, wf_hbm, we_hbm,
    draft_ref, ns_hbm,
    state_v, ns_v, wo, wf, we, em_own, em, g_buf, snd, r1, s_sum, s_snd, r2, feat, q_buf, d_snd, d_rcv,
    ssq_own, ssq_rcv, sc_buf,
    loc_sem, sib_s, sib_r, ez_s, ez_r, ag_s, ag_r, sq_s, sq_r, sc_s, sc_r, rs_s, rs_r, fg_s, fg_r, xr_s, xr_r,
):
    row = lax.axis_index("row")
    z = lax.axis_index("tensor")
    core = lax.rem(row, 2)
    chip = row // 2
    cx = chip // 4
    cy = lax.rem(chip, 4)
    zl = lax.rem(z, 4)
    zh = z // 4
    sib = (row + 1 - 2 * core, z)

    def zp(d):
        return (row, lax.rem(z + (d + 16), 16))

    def xyp(dx, dy):
        return ((lax.rem(cx + (dx + 4), 4) * 4 + lax.rem(cy + (dy + 4), 4)) * 2 + core, z)

    xy_all = [(a, b) for a in range(4) for b in range(4) if (a, b) != (0, 0)]
    barrier = pltpu.get_barrier_semaphore()
    peers = [sib] + [zp(d) for d in range(1, 16)] + [xyp(a, b) for a, b in xy_all]
    for p in peers:
        pl.semaphore_signal(barrier, inc=1, device_id=p, device_id_type=MESH)

    def rc(src, dst, ss, rs, dev):
        c = pltpu.make_async_remote_copy(
            src_ref=src, dst_ref=dst, send_sem=ss, recv_sem=rs, device_id=dev, device_id_type=MESH
        )
        c.start()
        return c

    loc = []
    for i, (s, d) in enumerate(
        ((state_hbm, state_v), (wo_hbm, wo.at[0]), (we_hbm, we.at[0]), (wf_hbm, wf.at[0]))
    ):
        c = pltpu.make_async_copy(s, d, loc_sem.at[i])
        c.start()
        loc.append(c)

    em_own[...] = emb_ref[...].astype(f32).reshape(2, 32, 256).astype(bf16)
    em[zl, zh, 0] = em_own[core]

    pl.semaphore_wait(barrier, len(peers))
    pend = []
    c_em = rc(em_own.at[1 - core], em.at[zl, zh, 1], sib_s.at[0], sib_r.at[0], sib)
    c_wo = rc(wo_hbm, wo.at[1], sib_s.at[1], sib_r.at[1], sib)
    c_we = rc(we_hbm, we.at[1], sib_s.at[2], sib_r.at[2], sib)
    c_wf = rc(wf_hbm, wf.at[1], sib_s.at[3], sib_r.at[3], sib)
    pend += [c_em, c_wo, c_we, c_wf]

    c_em.wait_recv()
    em_far = [
        rc(em.at[zl, zh], em.at[zl, zh], ez_s.at[m], ez_r.at[m], zp(4 * m)) for m in (2, 1, 3)
    ]
    pend += em_far

    x3 = x_ref[...].astype(f32)
    c3 = c_ref[...].astype(f32)
    b3 = b_ref[...].astype(f32)
    lane_head = lax.broadcasted_iota(jnp.int32, (8, 512), 1) // 64
    pick = (lane_head == lax.broadcasted_iota(jnp.int32, (8, 512), 0)).astype(f32)

    def expand(v):
        return jnp.dot(v, pick, precision=lax.Precision.HIGHEST, preferred_element_type=f32)

    step = jax.nn.softplus(logit_ref[...].reshape(32, 8) + bias_ref[...])
    step_x = expand(step)
    decay_x = expand(jnp.broadcast_to(decay_ref[...], (8, 8)))[0:1]
    skip_x = expand(jnp.broadcast_to(skip_ref[...], (8, 8)))[0:1]
    log_x = -step_x * decay_x
    t_in = lax.rem(lax.broadcasted_iota(jnp.int32, (32, 512), 0), 8)
    for k in (1, 2, 4):
        log_x = log_x + jnp.where(t_in >= k, pltpu.roll(log_x, k, 0), 0.0)
    log3 = log_x.reshape(4, 8, 512)
    step3 = step_x.reshape(4, 8, 512)
    sx3 = step3 * x3
    t3 = lax.broadcasted_iota(jnp.int32, (4, 8, 512), 1)
    gmat = [nt_dot(c3[r].astype(bf16), b3[r].astype(bf16)) for r in range(4)]
    intra = skip_x * x3
    for s in range(8):
        keep = t3 >= s
        e = jnp.where(keep, jnp.exp(jnp.where(keep, log3 - log3[:, s : s + 1, :], 0.0)), 0.0)
        gcol = jnp.stack([gmat[r][:, s : s + 1] for r in range(4)], axis=0)
        intra = intra + e * gcol * sx3[:, s : s + 1, :]
    loc[0].wait()
    carried = jnp.stack([nt_dot(c3[r].astype(bf16), state_v[r]) for r in range(4)], axis=0)
    mixed = jnp.exp(log3) * carried + intra
    gate = gate_ref[...].astype(f32)
    gated = (mixed * (gate / (1.0 + jnp.exp(-gate)))).reshape(32, 512)
    g_buf[0, 0] = (gated * gain_ref[...]).astype(bf16)
    ag = {}
    for a, b in xy_all:
        i = a * 4 + b
        ag[i] = rc(g_buf.at[0, 0], g_buf.at[a, b], ag_s.at[i], ag_r.at[i], xyp(a, b))
    ssq = jnp.sum(gated * gated, axis=1, keepdims=True)
    eye = lax.broadcasted_iota(jnp.int32, (32, 128), 0) == lax.broadcasted_iota(jnp.int32, (32, 128), 1)
    ssq_own[...] = jnp.sum(jnp.where(eye, ssq, 0.0), axis=0, keepdims=True)
    sq = [rc(ssq_own, ssq_rcv.at[d], sq_s.at[d], sq_r.at[d], zp(d)) for d in range(1, 16)]

    for r in range(4):
        k = acc_ref[r]
        t2 = t3[r]
        end = jnp.sum(jnp.where(t2 == k - 1, log3[r], 0.0), axis=0, keepdims=True)
        kept = t2 < k
        w = jnp.where(kept, jnp.exp(jnp.where(kept, end - log3[r], 0.0)), 0.0) * sx3[r]
        hi, mid, lo = split3(w)
        turned = jnp.transpose(
            jnp.concatenate([hi, mid, lo, jnp.broadcast_to(jnp.exp(end), (8, 512))], axis=0)
        )
        b24 = jnp.concatenate([b3[r], b3[r], b3[r]], axis=0).astype(bf16)
        add = jnp.dot(turned[:, 0:24].astype(bf16), b24, preferred_element_type=f32)
        ns_v[r] = (turned[:, 24:25] * state_v[r].astype(f32) + add).astype(bf16)
    ns_out = pltpu.make_async_copy(ns_v, ns_hbm, loc_sem.at[4])
    ns_out.start()

    for c in em_far:
        c.wait_recv()
    em_near = [
        rc(em.at[zl], em.at[zl], ez_s.at[4], ez_r.at[4], zp(1)),
        rc(em.at[zl], em.at[zl], ez_s.at[5], ez_r.at[5], zp(-1)),
        rc(em.at[zl, pl.ds(0, 2)], em.at[zl, pl.ds(0, 2)], ez_s.at[6], ez_r.at[6], zp(2)),
        rc(em.at[zl, pl.ds(2, 2)], em.at[zl, pl.ds(2, 2)], ez_s.at[7], ez_r.at[7], zp(-2)),
    ]
    pend += em_near

    for c in ag.values():
        c.wait_recv()
    loc[1].wait()
    c_wo.wait_recv()
    near = []
    for j, d in enumerate((2, 1, -1, 0)):
        g = g_buf[lax.rem(z + (d + 4), 4)].reshape(128, 512)
        for h in range(2):
            part = jnp.dot(g, wo[h], preferred_element_type=f32).reshape(4, 32, 256)
            cols = pl.ds(256 * h, 256)
            if d == 0:
                s_sum[:, :, cols] = part
            else:
                snd[j, :, :, cols] = part.astype(bf16)
        if d == 2:
            for h, dd in ((0, 2), (1, -2)):
                cols = pl.ds(256 * h, 256)
                near.append(
                    rc(snd.at[0, :, :, cols], r1.at[0, :, :, cols], rs_s.at[h], rs_r.at[h], zp(dd))
                )
        elif d != 0:
            near.append(rc(snd.at[j], r1.at[j], rs_s.at[1 + j], rs_r.at[1 + j], zp(d)))
    pend += near

    total = ssq_own[...]
    for c in sq:
        c.wait_recv()
    for d in range(1, 16):
        total = total + ssq_rcv[d]
    sc_buf[0] = lax.rsqrt(total / 8192.0 + norm_eps)
    sc = [
        rc(sc_buf.at[0], sc_buf.at[a * 4 + b], sc_s.at[a * 4 + b], sc_r.at[a * 4 + b], xyp(a, b))
        for a, b in xy_all
    ]
    pend += sq + sc + list(ag.values())

    for c in near:
        c.wait_recv()
    s_sum[...] = s_sum[...] + r1[0].astype(f32) + r1[1].astype(f32) + r1[2].astype(f32)
    s_snd[...] = s_sum[...].astype(bf16)
    far = []
    for m in (2, 1, 3):
        far.append(
            rc(s_snd.at[lax.rem(zh + m, 4)], r2.at[m], rs_s.at[4 + m], rs_r.at[4 + m], zp(4 * m))
        )
    pend += far

    loc[2].wait()
    c_we.wait_recv()
    for c in em_near:
        c.wait_recv()
    for a in range(4):
        ex = lax.rem(cx + (4 - a), 4)
        es = [em[lax.rem(cy + (4 - b), 4), ex] for b in range(4)]
        q = 0.0
        for h in range(2):
            e = jnp.concatenate([v[h] for v in es], axis=0)
            q = q + jnp.dot(e, we[h], preferred_element_type=f32)
        q_buf[a] = q.reshape(4, 32, 512)

    for c in far:
        c.wait_recv()
    feat[zl, zh] = (
        s_sum[zh] + r2[1].astype(f32) + r2[2].astype(f32) + r2[3].astype(f32)
    ).astype(bf16)
    f_far = [
        rc(feat.at[zl, zh], feat.at[zl, zh], fg_s.at[m], fg_r.at[m], zp(4 * m)) for m in (2, 1, 3)
    ]
    loc[3].wait()
    c_wf.wait_recv()
    for c in sc:
        c.wait_recv()
    for c in f_far:
        c.wait_recv()
    f_near = [
        rc(feat.at[zl, pl.ds(0, 2)], feat.at[zl, pl.ds(0, 2)], fg_s.at[6], fg_r.at[6], zp(2)),
        rc(feat.at[zl, pl.ds(2, 2)], feat.at[zl, pl.ds(2, 2)], fg_s.at[7], fg_r.at[7], zp(-2)),
        rc(feat.at[zl], feat.at[zl], fg_s.at[4], fg_r.at[4], zp(1)),
        rc(feat.at[zl], feat.at[zl], fg_s.at[5], fg_r.at[5], zp(-1)),
    ]
    pend += f_far + f_near
    for c in f_near:
        c.wait_recv()

    xr = []
    mine = None
    for a in (3, 2, 1, 0):
        f = feat[a].reshape(128, 512)
        y = jnp.dot(f[:, 0:256], wf[0], preferred_element_type=f32)
        y = y + jnp.dot(f[:, 256:512], wf[1], preferred_element_type=f32)
        for b in range(4):
            i = a * 4 + b
            scale = jnp.sum(jnp.where(eye, sc_buf[i], 0.0), axis=1, keepdims=True)
            out = y[32 * b : 32 * b + 32] * scale + q_buf[a, b]
            if i == 0:
                mine = out
            else:
                d_snd[a, b] = out.astype(bf16)
                xr.append(rc(d_snd.at[a, b], d_rcv.at[a, b], xr_s.at[i], xr_r.at[i], xyp(-a, -b)))
    for c in xr:
        c.wait_recv()
    for a, b in xy_all:
        mine = mine + d_rcv[a, b].astype(f32)
    mine = mine.reshape(4, 8, 512)
    for r in range(4):
        draft_ref[r] = jnp.where(t3[r] <= acc_ref[r], mine[r], 0.0).astype(bf16)
    ns_out.wait()
    for c in pend + xr:
        c.wait_send()


def body(
    ssm_input, gate_input, write_vectors, read_vectors, step_logit, step_bias, decay_rate, skip_gain,
    norm_gain, ssm_state, accepted, out_weight, token_embeds, feat_weight, embed_weight,
):
    vm = pl.BlockSpec(memory_space=pltpu.VMEM)
    hbm = pl.BlockSpec(memory_space=pl.ANY)
    dma = pltpu.SemaphoreType.DMA
    draft, new_state = pl.pallas_call(
        kernel,
        out_shape=(
            jax.ShapeDtypeStruct((4, 8, 512), bf16),
            jax.ShapeDtypeStruct((4, 512, 256), bf16),
        ),
        in_specs=[vm] * 9 + [pl.BlockSpec(memory_space=pltpu.SMEM), vm] + [hbm] * 4,
        out_specs=(vm, hbm),
        scratch_shapes=[
            pltpu.VMEM((4, 512, 256), bf16),
            pltpu.VMEM((4, 512, 256), bf16),
            pltpu.VMEM((2, 512, 256), bf16),
            pltpu.VMEM((2, 256, 512), bf16),
            pltpu.VMEM((2, 256, 512), bf16),
            pltpu.VMEM((2, 32, 256), bf16),
            pltpu.VMEM((4, 4, 2, 32, 256), bf16),
            pltpu.VMEM((4, 4, 32, 512), bf16),
            pltpu.VMEM((3, 4, 32, 512), bf16),
            pltpu.VMEM((3, 4, 32, 512), bf16),
            pltpu.VMEM((4, 32, 512), f32),
            pltpu.VMEM((4, 32, 512), bf16),
            pltpu.VMEM((4, 32, 512), bf16),
            pltpu.VMEM((4, 4, 32, 512), bf16),
            pltpu.VMEM((4, 4, 32, 512), f32),
            pltpu.VMEM((4, 4, 32, 512), bf16),
            pltpu.VMEM((4, 4, 32, 512), bf16),
            pltpu.VMEM((1, 128), f32),
            pltpu.VMEM((16, 1, 128), f32),
            pltpu.VMEM((16, 1, 128), f32),
            dma((5,)),
            dma((4,)), dma((4,)),
            dma((8,)), dma((8,)),
            dma((16,)), dma((16,)),
            dma((16,)), dma((16,)),
            dma((16,)), dma((16,)),
            dma((8,)), dma((8,)),
            dma((8,)), dma((8,)),
            dma((16,)), dma((16,)),
        ],
        compiler_params=pltpu.CompilerParams(
            collective_id=0, has_side_effects=True, vmem_limit_bytes=40 * 1024 * 1024
        ),
        name="verify_step",
    )(
        ssm_input, gate_input, write_vectors, read_vectors, step_logit,
        step_bias.reshape(1, 8), decay_rate.reshape(1, 8), skip_gain.reshape(1, 8),
        norm_gain.reshape(1, 512), accepted, token_embeds,
        ssm_state.reshape(4, 512, 256), out_weight, feat_weight, embed_weight,
    )
    return draft, new_state.reshape(4, 8, 64, 256)


def solution(mesh):
    in_specs = (
        P("row", None, "tensor"),
        P("row", None, "tensor"),
        P("row", None, "tensor"),
        P("row", None, "tensor"),
        P("row", None, "tensor"),
        P("tensor"),
        P("tensor"),
        P("tensor"),
        P("tensor"),
        P("row", "tensor", None, None),
        P("row"),
        P("tensor", "row"),
        P("tensor", None, "row"),
        P("row", "tensor"),
        P("row", "tensor"),
    )
    out_specs = (P("row", None, "tensor"), P("row", "tensor", None, None))
    return jax.shard_map(body, mesh=mesh, in_specs=in_specs, out_specs=out_specs, check_vma=False)
```

```python
import functools

import jax
import jax.numpy as jnp
from jax import lax
from jax.experimental import pallas as pl
from jax.experimental.pallas import tpu as pltpu
from jax.sharding import PartitionSpec as P

norm_eps = 1e-05
MESH = pl.DeviceIdType.MESH
f32 = jnp.float32
bf16 = jnp.bfloat16


def nt_dot(a, b):
    return lax.dot_general(a, b, (((1,), (1,)), ((), ())), preferred_element_type=f32)


def split3(v):
    hi = v.astype(bf16).astype(f32)
    mid = (v - hi).astype(bf16).astype(f32)
    return hi, mid, v - hi - mid


def kernel(
    x_hbm, gate_hbm, b_hbm, c_hbm, logit_hbm, bias_hbm, decay_hbm, skip_hbm, gain_hbm, state_hbm, acc_hbm,
    wo_hbm, emb_hbm, wf_hbm, we_hbm,
    draft_hbm, ns_hbm,
    x_ref, gate_ref, b_ref, c_ref, logit_ref, bias_ref, decay_ref, skip_ref, gain_ref, acc_ref, emb_ref,
    draft_ref, ns_ref, state_v, wo, wf, we, em_own, em, g_buf, p_own, p_snd, r1, s_snd, r2, feat, q_buf, d_snd, d_rcv,
    ssq_own, ssq_rcv, sc_buf,
    loc_sem, sib_s, sib_r, ez_s, ez_r, en_s, en_r, ag_s, ag_r, sq_s, sq_r, sc_s, sc_r, rs_s, rs_r,
    rf_s, rf_r, ff_s, ff_r, fn_s, fn_r, xr_s, xr_r,
):
    groups = (6, -6, 3, -3, 0)
    slot = {g: i for i, g in enumerate(groups)}
    row = lax.axis_index("row")
    z = lax.axis_index("tensor")
    core = lax.rem(row, 2)
    chip = row // 2
    cx = chip // 4
    cy = lax.rem(chip, 4)
    sib = (row + 1 - 2 * core, z)

    def at(d):
        return lax.rem(z + (d + 16), 16)

    def zp(d):
        return (row, at(d))

    def xyp(dx, dy):
        return ((lax.rem(cx + (dx + 4), 4) * 4 + lax.rem(cy + (dy + 4), 4)) * 2 + core, z)

    xy_all = [(a, b) for a in range(4) for b in range(4) if (a, b) != (0, 0)]
    barrier = pltpu.get_barrier_semaphore()
    peers = [sib] + [(sib[0], at(d)) for d in (6, -6, 3, -3)] + [zp(d) for d in range(1, 16)] + [xyp(a, b) for a, b in xy_all]
    for p in peers:
        pl.semaphore_signal(barrier, inc=1, device_id=p, device_id_type=MESH)

    def rc(src, dst, ss, rs, dev):
        c = pltpu.make_async_remote_copy(
            src_ref=src, dst_ref=dst, send_sem=ss, recv_sem=rs, device_id=dev, device_id_type=MESH
        )
        c.start()
        return c

    def wait_arrival(ref, sem):
        pltpu.make_async_remote_copy(
            src_ref=ref, dst_ref=ref, send_sem=sem, recv_sem=sem, device_id=sib, device_id_type=MESH
        ).wait_recv()

    def wait_leave(ref, sem):
        pltpu.make_async_remote_copy(
            src_ref=ref, dst_ref=ref, send_sem=sem, recv_sem=sem, device_id=sib, device_id_type=MESH
        ).wait_send()

    loc = []
    for i, (s, d) in enumerate(
        (
            (emb_hbm, emb_ref), (logit_hbm, logit_ref), (bias_hbm, bias_ref), (decay_hbm, decay_ref),
            (skip_hbm, skip_ref), (acc_hbm, acc_ref), (x_hbm, x_ref), (c_hbm, c_ref), (b_hbm, b_ref),
            (gate_hbm, gate_ref), (gain_hbm, gain_ref), (state_hbm, state_v), (wo_hbm, wo.at[0]),
            (we_hbm, we.at[0]), (wf_hbm, wf.at[0]),
        )
    ):
        c = pltpu.make_async_copy(s, d, loc_sem.at[i])
        c.start()
        loc.append(c)
    loc_wo, loc_we, loc_wf = loc[12:]

    loc[0].wait()
    em_own[...] = emb_ref[...].astype(f32).reshape(2, 32, 256).astype(bf16)
    em[z, 0] = em_own[core]

    for c in loc[1:11]:
        c.wait()
    x3 = x_ref[...].astype(f32)
    c3 = c_ref[...].astype(f32)
    b3 = b_ref[...].astype(f32)
    lane_head = lax.broadcasted_iota(jnp.int32, (8, 512), 1) // 64
    pick = (lane_head == lax.broadcasted_iota(jnp.int32, (8, 512), 0)).astype(f32)
    bias = jnp.zeros((1, 8), f32)
    decay_x = jnp.zeros((1, 512), f32)
    skip_x = jnp.zeros((1, 512), f32)
    for h in range(8):
        bias = jnp.where(lax.broadcasted_iota(jnp.int32, (1, 8), 1) == h, bias_ref[h], bias)
        decay_x = jnp.where(lane_head[0:1] == h, decay_ref[h], decay_x)
        skip_x = jnp.where(lane_head[0:1] == h, skip_ref[h], skip_x)

    def expand(v):
        return jnp.dot(v, pick, precision=lax.Precision.HIGHEST, preferred_element_type=f32)

    step = jax.nn.softplus(logit_ref[...].reshape(32, 8) + bias)
    step_x = expand(step)
    log_x = -step_x * decay_x
    t_in = lax.rem(lax.broadcasted_iota(jnp.int32, (32, 512), 0), 8)
    for k in (1, 2, 4):
        log_x = log_x + jnp.where(t_in >= k, pltpu.roll(log_x, k, 0), 0.0)
    log3 = log_x.reshape(4, 8, 512)
    step3 = step_x.reshape(4, 8, 512)
    sx3 = step3 * x3
    t3 = lax.broadcasted_iota(jnp.int32, (4, 8, 512), 1)
    gmat = [nt_dot(c3[r].astype(bf16), b3[r].astype(bf16)) for r in range(4)]
    intra = skip_x * x3
    for s in range(8):
        keep = t3 >= s
        e = jnp.where(keep, jnp.exp(jnp.where(keep, log3 - log3[:, s : s + 1, :], 0.0)), 0.0)
        gcol = jnp.stack([gmat[r][:, s : s + 1] for r in range(4)], axis=0)
        intra = intra + e * gcol * sx3[:, s : s + 1, :]
    loc[11].wait()
    carried = jnp.stack([nt_dot(c3[r].astype(bf16), state_v[r]) for r in range(4)], axis=0)
    mixed = jnp.exp(log3) * carried + intra
    gate = gate_ref[...].astype(f32)
    gated = (mixed * (gate / (1.0 + jnp.exp(-gate)))).reshape(32, 512)
    g_buf[0] = (gated * gain_ref[...].reshape(1, 512)).astype(bf16)
    ssq = jnp.sum(gated * gated, axis=1, keepdims=True)
    eye = lax.broadcasted_iota(jnp.int32, (32, 128), 0) == lax.broadcasted_iota(jnp.int32, (32, 128), 1)
    ssq_own[...] = jnp.sum(jnp.where(eye, ssq, 0.0), axis=0, keepdims=True)

    pl.semaphore_wait(barrier, len(peers))
    def normed_send(o, i):
        rc(g_buf.at[0], g_buf.at[o], ag_s.at[0], ag_r.at[i], xyp(o // 4, lax.rem(o, 4)))

    members = {g: (-1, 0, 1, 2) if g == 6 else (-1, 0, 1) for g in groups}
    for g in groups:
        for d in members[g]:
            o = at(g + d)
            pl.when(o != 0)(functools.partial(normed_send, o, slot[g]))
    c_em = rc(em_own.at[1 - core], em.at[z, 1], sib_s.at[0], sib_r.at[0], sib)
    c_wo = rc(wo_hbm, wo.at[1], sib_s.at[1], sib_r.at[1], sib)
    c_we = rc(we_hbm, we.at[1], sib_s.at[2], sib_r.at[2], sib)
    c_wf = rc(wf_hbm, wf.at[1], sib_s.at[3], sib_r.at[3], sib)

    for g in (6, -6, 3, -3):
        rc(em_own.at[core], em.at[z, 0], ez_s.at[0], ez_r.at[0], zp(g))
        rc(em_own.at[1 - core], em.at[z, 1], ez_s.at[0], ez_r.at[0], (sib[0], at(g)))

    def embeds_near(g):
        o = at(-g)
        if g == 6:
            rc(em.at[o, 0], em.at[o, 0], en_s.at[1], en_r.at[1], zp(2))
        if g == -6:
            rc(em.at[o, 1], em.at[o, 1], en_s.at[2], en_r.at[2], zp(-2))
        rc(em.at[o], em.at[o], en_s.at[0], en_r.at[0], zp(1))
        rc(em.at[o], em.at[o], en_s.at[0], en_r.at[0], zp(-1))

    for d in range(1, 16):
        rc(ssq_own, ssq_rcv.at[d], sq_s.at[0], sq_r.at[0], zp(d))
    c_em.wait_recv()
    embeds_near(0)

    for r in range(4):
        k = acc_ref[r]
        t2 = t3[r]
        end = jnp.sum(jnp.where(t2 == k - 1, log3[r], 0.0), axis=0, keepdims=True)
        kept = t2 < k
        w = jnp.where(kept, jnp.exp(jnp.where(kept, end - log3[r], 0.0)), 0.0) * sx3[r]
        hi, mid, lo = split3(w)
        turned = jnp.transpose(
            jnp.concatenate([hi, mid, lo, jnp.broadcast_to(jnp.exp(end), (8, 512))], axis=0)
        )
        b24 = jnp.concatenate([b3[r], b3[r], b3[r]], axis=0).astype(bf16)
        add = jnp.dot(turned[:, 0:24].astype(bf16), b24, preferred_element_type=f32)
        ns_ref[r] = (turned[:, 24:25] * state_v[r].astype(f32) + add).astype(bf16)
    ns_out = pltpu.make_async_copy(ns_ref, ns_hbm, loc_sem.at[15])
    ns_out.start()

    loc_wo.wait()
    c_wo.wait_recv()
    for g in groups:
        i = slot[g]
        n = len(members[g])
        own_inside = functools.reduce(jnp.logical_or, [at(g + d) == 0 for d in members[g]])
        pl.when(own_inside)(lambda n=n, i=i: wait_arrival(g_buf.at[pl.ds(0, n - 1)], ag_r.at[i]))
        pl.when(jnp.logical_not(own_inside))(lambda n=n, i=i: wait_arrival(g_buf.at[pl.ds(0, n)], ag_r.at[i]))
        rows = jnp.concatenate([g_buf[at(g + d)] for d in members[g]], axis=0)
        for h in range(2):
            part = jnp.dot(rows, wo[h], preferred_element_type=f32).reshape(n, 32, 256)
            cols = pl.ds(256 * h, 256)
            p_own[i, :, cols] = part[1]
            p_snd[i, 0:n, :, cols] = part.astype(bf16)
        rc(p_snd.at[i, 2], r1.at[i, 0], rs_s.at[0], rs_r.at[i], zp(1))
        rc(p_snd.at[i, 0], r1.at[i, 1], rs_s.at[0], rs_r.at[i], zp(-1))
        if g == 6:
            cols = pl.ds(0, 256)
            rc(p_snd.at[0, 3, :, cols], r1.at[i, 2, :, cols], rs_s.at[1], rs_r.at[5], zp(2))
        if g == -6:
            cols = pl.ds(256, 256)
            rc(p_snd.at[0, 3, :, cols], r1.at[i, 2, :, cols], rs_s.at[2], rs_r.at[6], zp(-2))

    for g in groups:
        i = slot[g]
        wait_arrival(r1.at[i, pl.ds(0, 2)], rs_r.at[i])
        p_own[i] = p_own[i] + r1[i, 0].astype(f32) + r1[i, 1].astype(f32)
        if abs(g) == 6:
            cols = pl.ds(0 if g > 0 else 256, 256)
            wait_arrival(r1.at[i, 2, :, cols], rs_r.at[5 if g > 0 else 6])
            p_own[i, :, cols] = p_own[i, :, cols] + r1[i, 2, :, cols].astype(f32)
        if g != 0:
            s_snd[i] = p_own[i].astype(bf16)
            rc(s_snd.at[i], r2.at[i], rf_s.at[0], rf_r.at[0], zp(g))

    wait_arrival(em.at[pl.ds(0, 4)], ez_r.at[0])
    for g in (6, -6, 3, -3):
        embeds_near(g)

    total = ssq_own[...]
    wait_arrival(ssq_rcv.at[pl.ds(1, 15)], sq_r.at[0])
    for d in range(1, 16):
        total = total + ssq_rcv[d]
    sc_buf[0] = lax.rsqrt(total / 8192.0 + norm_eps)
    for a, b in xy_all:
        rc(sc_buf.at[0], sc_buf.at[a * 4 + b], sc_s.at[0], sc_r.at[0], xyp(a, b))

    wait_arrival(r2, rf_r.at[0])
    total = p_own[slot[0]]
    for g in (3, -3, 6, -6):
        total = total + r2[slot[g]].astype(f32)
    feat[z] = total.astype(bf16)
    f_far = {}
    for g in (6, -6, 3, -3):
        f_far[g] = rc(feat.at[z], feat.at[z], ff_s.at[0], ff_r.at[slot[g]], zp(g))

    def forward(g):
        c = feat.at[at(-g)]
        if abs(g) == 6:
            h = 0 if g > 0 else 1
            half = feat.at[at(-g), :, pl.ds(256 * h, 256)]
            rc(half, half, fn_s.at[1 + h], fn_r.at[5 + h], zp(2 if g > 0 else -2))
        rc(c, c, fn_s.at[0], fn_r.at[slot[g]], zp(1))
        rc(c, c, fn_s.at[0], fn_r.at[slot[g]], zp(-1))

    forward(0)

    loc_wf.wait()
    c_wf.wait_recv()
    wait_arrival(sc_buf.at[pl.ds(1, 15)], sc_r.at[0])

    def draft_send(o):
        rc(d_snd.at[o], d_rcv.at[o], xr_s.at[0], xr_r.at[0], xyp(-(o // 4), -lax.rem(o, 4)))

    def project(deltas):
        f = jnp.concatenate([feat[at(d)] for d in deltas], axis=0)
        y = jnp.dot(f[:, 0:256], wf[0], preferred_element_type=f32)
        y = y + jnp.dot(f[:, 256:512], wf[1], preferred_element_type=f32)
        for i, d in enumerate(deltas):
            o = at(d)
            scale = jnp.sum(jnp.where(eye, sc_buf[o], 0.0), axis=1, keepdims=True)
            out = y[32 * i : 32 * i + 32] * scale + q_buf[o]
            q_buf[o] = out
            d_snd[o] = out.astype(bf16)
            pl.when(o != 0)(functools.partial(draft_send, o))

    for g in (3, -3):
        i = slot[g]
        f_far[g].wait_recv()
        forward(g)
    loc_we.wait()
    c_we.wait_recv()
    wait_arrival(em.at[pl.ds(0, 10)], en_r.at[0])
    wait_arrival(em.at[0, 0], en_r.at[1])
    wait_arrival(em.at[0, 1], en_r.at[2])
    for a in range(4):
        es = [em[lax.rem(cx + (4 - a), 4) * 4 + lax.rem(cy + (4 - b), 4)] for b in range(4)]
        q = 0.0
        for h in range(2):
            e = jnp.concatenate([v[h] for v in es], axis=0)
            q = q + jnp.dot(e, we[h], preferred_element_type=f32)
        q_buf[4 * a : 4 * a + 4] = q.reshape(4, 32, 512)
    for g in (6, -6):
        i = slot[g]
        f_far[g].wait_recv()
        forward(g)
    for g, deltas in (
        (0, (-1, 0, 1)), (3, (-4, -3, -2)), (-3, (2, 3, 4)), (6, (-7, -6, -5)), (-6, (5, 6, 7, 8))
    ):
        i = slot[g]
        wait_arrival(feat.at[pl.ds(0, 2)], fn_r.at[i])
        if g == -6:
            wait_arrival(feat.at[0, :, pl.ds(0, 256)], fn_r.at[5])
            wait_arrival(feat.at[0, :, pl.ds(256, 256)], fn_r.at[6])
        project(deltas)

    wait_arrival(d_rcv.at[pl.ds(1, 15)], xr_r.at[0])
    mine = q_buf[0]
    for o in range(1, 16):
        mine = mine + d_rcv[o].astype(f32)
    mine = mine.reshape(4, 8, 512)
    for r in range(4):
        draft_ref[r] = jnp.where(t3[r] <= acc_ref[r], mine[r], 0.0).astype(bf16)
    draft_out = pltpu.make_async_copy(draft_ref, draft_hbm, loc_sem.at[16])
    draft_out.start()
    ns_out.wait()
    for c in (c_em, c_wo, c_we, c_wf):
        c.wait_send()
    chunk_half = feat.at[0, :, pl.ds(0, 256)]
    wait_leave(g_buf.at[pl.ds(1, 15)], ag_s.at[0])
    wait_leave(em.at[pl.ds(0, 4)], ez_s.at[0])
    wait_leave(em.at[pl.ds(0, 10)], en_s.at[0])
    wait_leave(ssq_rcv.at[pl.ds(1, 15)], sq_s.at[0])
    wait_leave(sc_buf.at[pl.ds(1, 15)], sc_s.at[0])
    wait_leave(feat.at[pl.ds(0, 10)], rs_s.at[0])
    wait_leave(r2, rf_s.at[0])
    wait_leave(feat.at[pl.ds(0, 4)], ff_s.at[0])
    wait_leave(feat.at[pl.ds(0, 10)], fn_s.at[0])
    wait_leave(d_rcv.at[pl.ds(1, 15)], xr_s.at[0])
    for sems in (en_s, rs_s, fn_s):
        wait_leave(chunk_half, sems.at[1])
        wait_leave(chunk_half, sems.at[2])
    draft_out.wait()


def finish(draft_in, ns_in, draft_out, ns_out, draft_v, ns_v, sem):
    def moves(i):
        if i == 4:
            return (draft_in, draft_v, sem.at[4]), (draft_v, draft_out, sem.at[9])
        return (ns_in.at[i], ns_v.at[i], sem.at[i]), (ns_v.at[i], ns_out.at[i], sem.at[5 + i])

    arrive = [pltpu.make_async_copy(*moves(i)[0]) for i in range(5)]
    leave = [pltpu.make_async_copy(*moves(i)[1]) for i in range(5)]
    for c in arrive:
        c.start()
    for c, d in zip(arrive, leave):
        c.wait()
        d.start()
    for d in leave:
        d.wait()


def body(
    ssm_input, gate_input, write_vectors, read_vectors, step_logit, step_bias, decay_rate, skip_gain,
    norm_gain, ssm_state, accepted, out_weight, token_embeds, feat_weight, embed_weight,
):
    hbm = pl.BlockSpec(memory_space=pltpu.HBM)
    dma = pltpu.SemaphoreType.DMA
    draft, new_state = pl.pallas_call(
        kernel,
        out_shape=(
            jax.ShapeDtypeStruct((4, 8, 512), bf16),
            jax.ShapeDtypeStruct((4, 512, 256), bf16),
        ),
        in_specs=[hbm] * 15,
        out_specs=(hbm, hbm),
        scratch_shapes=[
            pltpu.VMEM((4, 8, 512), bf16),
            pltpu.VMEM((4, 8, 512), bf16),
            pltpu.VMEM((4, 8, 256), bf16),
            pltpu.VMEM((4, 8, 256), bf16),
            pltpu.VMEM((4, 8, 8), f32),
            pltpu.SMEM((8,), f32),
            pltpu.SMEM((8,), f32),
            pltpu.SMEM((8,), f32),
            pltpu.VMEM((512,), f32),
            pltpu.SMEM((4,), jnp.int32),
            pltpu.VMEM((8, 8, 256), bf16),
            pltpu.VMEM((4, 8, 512), bf16),
            pltpu.VMEM((4, 512, 256), bf16),
            pltpu.VMEM((4, 512, 256), bf16),
            pltpu.VMEM((2, 512, 256), bf16),
            pltpu.VMEM((2, 256, 512), bf16),
            pltpu.VMEM((2, 256, 512), bf16),
            pltpu.VMEM((2, 32, 256), bf16),
            pltpu.VMEM((16, 2, 32, 256), bf16),
            pltpu.VMEM((16, 32, 512), bf16),
            pltpu.VMEM((5, 32, 512), f32),
            pltpu.VMEM((5, 4, 32, 512), bf16),
            pltpu.VMEM((5, 3, 32, 512), bf16),
            pltpu.VMEM((4, 32, 512), bf16),
            pltpu.VMEM((4, 32, 512), bf16),
            pltpu.VMEM((16, 32, 512), bf16),
            pltpu.VMEM((16, 32, 512), f32),
            pltpu.VMEM((16, 32, 512), bf16),
            pltpu.VMEM((16, 32, 512), bf16),
            pltpu.VMEM((1, 128), f32),
            pltpu.VMEM((16, 1, 128), f32),
            pltpu.VMEM((16, 1, 128), f32),
            dma((17,)),
            dma((4,)), dma((4,)),
            dma((1,)), dma((1,)),
            dma((3,)), dma((3,)),
            dma((1,)), dma((5,)),
            dma((1,)), dma((1,)),
            dma((1,)), dma((1,)),
            dma((3,)), dma((7,)),
            dma((1,)), dma((1,)),
            dma((1,)), dma((4,)),
            dma((3,)), dma((7,)),
            dma((1,)), dma((1,)),
        ],
        compiler_params=pltpu.CompilerParams(
            collective_id=0, has_side_effects=True, vmem_limit_bytes=56 * 1024 * 1024
        ),
        name="verify_step",
    )(
        ssm_input, gate_input, write_vectors, read_vectors, step_logit, step_bias, decay_rate, skip_gain,
        norm_gain, ssm_state.reshape(4, 512, 256), accepted, out_weight, token_embeds, feat_weight, embed_weight,
    )
    draft, new_state = pl.pallas_call(
        finish,
        out_shape=(
            jax.ShapeDtypeStruct((4, 8, 512), bf16),
            jax.ShapeDtypeStruct((4, 512, 256), bf16),
        ),
        in_specs=[hbm] * 2,
        out_specs=(hbm, hbm),
        scratch_shapes=[pltpu.VMEM((4, 8, 512), bf16), pltpu.VMEM((4, 512, 256), bf16), dma((10,))],
        name="results",
    )(draft, new_state)
    return draft, new_state.reshape(4, 8, 64, 256)


def solution(mesh):
    in_specs = (
        P("row", None, "tensor"),
        P("row", None, "tensor"),
        P("row", None, "tensor"),
        P("row", None, "tensor"),
        P("row", None, "tensor"),
        P("tensor"),
        P("tensor"),
        P("tensor"),
        P("tensor"),
        P("row", "tensor", None, None),
        P("row"),
        P("tensor", "row"),
        P("tensor", None, "row"),
        P("row", "tensor"),
        P("row", "tensor"),
    )
    out_specs = (P("row", None, "tensor"), P("row", "tensor", None, None))
    return jax.shard_map(body, mesh=mesh, in_specs=in_specs, out_specs=out_specs, check_vma=False)
```

```python
import functools

import jax
import jax.numpy as jnp
from jax import lax
from jax.experimental import pallas as pl
from jax.experimental.pallas import tpu as pltpu
from jax.sharding import PartitionSpec as P

norm_eps = 1e-05
MESH = pl.DeviceIdType.MESH
f32 = jnp.float32
bf16 = jnp.bfloat16


def nt_dot(a, b):
    return lax.dot_general(a, b, (((1,), (1,)), ((), ())), preferred_element_type=f32)


def split3(v):
    hi = v.astype(bf16).astype(f32)
    mid = (v - hi).astype(bf16).astype(f32)
    return hi, mid, v - hi - mid


def kernel(
    x_hbm, gate_hbm, b_hbm, c_hbm, logit_hbm, bias_hbm, decay_hbm, skip_hbm, gain_hbm, state_hbm, acc_hbm,
    wo_hbm, emb_hbm, wf_hbm, we_hbm,
    draft_hbm, ns_hbm,
    x_ref, gate_ref, b_ref, c_ref, logit_ref, bias_ref, decay_ref, skip_ref, gain_ref, acc_ref, emb_ref,
    draft_ref, ns_ref, state_v, wo, wf, we, em_own, em, g_buf, p_own, p_snd, r1, s_snd, r2, feat, q_buf, d_snd, d_rcv,
    ssq_own, ssq_snd, ssq_rcv, sc_buf,
    past_sem, loc_sem, sib_s, sib_r, ez_s, ez_r, en_s, en_r, ag_s, ag_r, sq_s, sq_r, sc_s, sc_r, rs_s, rs_r,
    rf_s, rf_r, ff_s, ff_r, fn_s, fn_r, xr_s, xr_r,
):
    groups = (6, -6, 3, -3, 0)
    slot = {g: i for i, g in enumerate(groups)}
    row = lax.axis_index("row")
    z = lax.axis_index("tensor")
    core = lax.rem(row, 2)
    chip = row // 2
    cx = chip // 4
    cy = lax.rem(chip, 4)
    sib = (row + 1 - 2 * core, z)

    def at(d):
        return lax.rem(z + (d + 16), 16)

    def zp(d):
        return (row, at(d))

    def xyp(dx, dy):
        return ((lax.rem(cx + (dx + 4), 4) * 4 + lax.rem(cy + (dy + 4), 4)) * 2 + core, z)

    def place(o):
        p = lax.rem(5 * o, 16)
        return p // 4, lax.rem(p, 4)

    xy_all = [(a, b) for a in range(4) for b in range(4) if (a, b) != (0, 0)]
    barrier = pltpu.get_barrier_semaphore()
    peers = [xyp(a, b) for a, b in sorted(xy_all, key=lambda p: -min(p[0], 4 - p[0]) - min(p[1], 4 - p[1]))]
    peers += [zp(3), zp(-3), (sib[0], at(3)), (sib[0], at(-3)), zp(2), zp(-2), zp(1), zp(-1), sib]
    for p in peers:
        pl.semaphore_signal(barrier, inc=1, device_id=p, device_id_type=MESH)

    def rc(src, dst, ss, rs, dev):
        c = pltpu.make_async_remote_copy(
            src_ref=src, dst_ref=dst, send_sem=ss, recv_sem=rs, device_id=dev, device_id_type=MESH
        )
        c.start()
        return c

    def wait_arrival(ref, sem):
        pltpu.make_async_remote_copy(
            src_ref=ref, dst_ref=ref, send_sem=sem, recv_sem=sem, device_id=sib, device_id_type=MESH
        ).wait_recv()

    def wait_leave(ref, sem):
        pltpu.make_async_remote_copy(
            src_ref=ref, dst_ref=ref, send_sem=sem, recv_sem=sem, device_id=sib, device_id_type=MESH
        ).wait_send()

    loc = []
    for i, (s, d) in enumerate(
        (
            (emb_hbm, emb_ref), (logit_hbm, logit_ref), (bias_hbm, bias_ref), (decay_hbm, decay_ref),
            (skip_hbm, skip_ref), (acc_hbm, acc_ref), (x_hbm, x_ref), (c_hbm, c_ref), (b_hbm, b_ref),
            (gate_hbm, gate_ref), (gain_hbm, gain_ref), (state_hbm, state_v), (wo_hbm, wo.at[0]),
            (we_hbm, we.at[0]), (wf_hbm, wf.at[0]),
        )
    ):
        c = pltpu.make_async_copy(s, d, loc_sem.at[i])
        c.start()
        loc.append(c)
    loc_wo, loc_we, loc_wf = loc[12:]

    loc[0].wait()
    em_own[...] = emb_ref[...].astype(f32).reshape(2, 32, 256).astype(bf16)
    em[z, 0] = em_own[core]

    for c in loc[1:11]:
        c.wait()
    x3 = x_ref[...].astype(f32)
    c3 = c_ref[...].astype(f32)
    b3 = b_ref[...].astype(f32)
    lane_head = lax.broadcasted_iota(jnp.int32, (8, 512), 1) // 64
    pick = (lane_head == lax.broadcasted_iota(jnp.int32, (8, 512), 0)).astype(f32)
    bias = jnp.zeros((1, 8), f32)
    decay_x = jnp.zeros((1, 512), f32)
    skip_x = jnp.zeros((1, 512), f32)
    for h in range(8):
        bias = jnp.where(lax.broadcasted_iota(jnp.int32, (1, 8), 1) == h, bias_ref[h], bias)
        decay_x = jnp.where(lane_head[0:1] == h, decay_ref[h], decay_x)
        skip_x = jnp.where(lane_head[0:1] == h, skip_ref[h], skip_x)

    def expand(v):
        return jnp.dot(v, pick, precision=lax.Precision.HIGHEST, preferred_element_type=f32)

    step = jax.nn.softplus(logit_ref[...].reshape(32, 8) + bias)
    step_x = expand(step)
    log_x = -step_x * decay_x
    t_in = lax.rem(lax.broadcasted_iota(jnp.int32, (32, 512), 0), 8)
    for k in (1, 2, 4):
        log_x = log_x + jnp.where(t_in >= k, pltpu.roll(log_x, k, 0), 0.0)
    log3 = log_x.reshape(4, 8, 512)
    step3 = step_x.reshape(4, 8, 512)
    sx3 = step3 * x3
    t3 = lax.broadcasted_iota(jnp.int32, (4, 8, 512), 1)
    gmat = [nt_dot(c3[r].astype(bf16), b3[r].astype(bf16)) for r in range(4)]
    intra = skip_x * x3
    for s in range(8):
        keep = t3 >= s
        e = jnp.where(keep, jnp.exp(jnp.where(keep, log3 - log3[:, s : s + 1, :], 0.0)), 0.0)
        gcol = jnp.stack([gmat[r][:, s : s + 1] for r in range(4)], axis=0)
        intra = intra + e * gcol * sx3[:, s : s + 1, :]
    loc[11].wait()
    carried = jnp.stack([nt_dot(c3[r].astype(bf16), state_v[r]) for r in range(4)], axis=0)
    mixed = jnp.exp(log3) * carried + intra
    gate = gate_ref[...].astype(f32)
    gated = (mixed * (gate / (1.0 + jnp.exp(-gate)))).reshape(32, 512)
    g_buf[0] = (gated * gain_ref[...].reshape(1, 512)).astype(bf16)
    ssq = jnp.sum(gated * gated, axis=1, keepdims=True)
    eye = lax.broadcasted_iota(jnp.int32, (32, 128), 0) == lax.broadcasted_iota(jnp.int32, (32, 128), 1)
    ssq_own[...] = jnp.sum(jnp.where(eye, ssq, 0.0), axis=0, keepdims=True)

    pl.semaphore_wait(barrier, len(peers))
    def normed_send(o, i):
        dx, dy = place(o)
        rc(g_buf.at[0], g_buf.at[o], ag_s.at[0], ag_r.at[i], xyp(dx, dy))

    members = {g: (-1, 0, 1, 2) if g == 6 else (-1, 0, 1) for g in groups}
    for g in groups:
        for d in members[g]:
            o = at(g + d)
            pl.when(o != 0)(functools.partial(normed_send, o, slot[g]))
    c_em = rc(em_own.at[1 - core], em.at[z, 1], sib_s.at[0], sib_r.at[0], sib)
    c_wo = rc(wo_hbm, wo.at[1], sib_s.at[1], sib_r.at[1], sib)
    c_we = rc(we_hbm, we.at[1], sib_s.at[2], sib_r.at[2], sib)
    c_wf = rc(wf_hbm, wf.at[1], sib_s.at[3], sib_r.at[3], sib)

    def embeds_far(g):
        rc(em_own.at[core], em.at[z, 0], ez_s.at[0], ez_r.at[0], zp(g))
        rc(em_own.at[1 - core], em.at[z, 1], ez_s.at[0], ez_r.at[0], (sib[0], at(g)))

    for g in (3, -3):
        pl.semaphore_signal(past_sem, inc=1, device_id=zp(g), device_id_type=MESH)
        embeds_far(g)

    def embeds_near(g):
        o = at(-g)
        if g == 6:
            rc(em.at[o, 0], em.at[o, 0], en_s.at[1], en_r.at[1], zp(2))
        if g == -6:
            rc(em.at[o, 1], em.at[o, 1], en_s.at[2], en_r.at[2], zp(-2))
        rc(em.at[o], em.at[o], en_s.at[0], en_r.at[0], zp(1))
        rc(em.at[o], em.at[o], en_s.at[0], en_r.at[0], zp(-1))

    for i, d in enumerate((1, -1, -2)):
        rc(ssq_own, ssq_rcv.at[i], sq_s.at[0], sq_r.at[0], zp(d))
    c_em.wait_recv()
    embeds_near(0)

    for r in range(4):
        k = acc_ref[r]
        t2 = t3[r]
        end = jnp.sum(jnp.where(t2 == k - 1, log3[r], 0.0), axis=0, keepdims=True)
        kept = t2 < k
        w = jnp.where(kept, jnp.exp(jnp.where(kept, end - log3[r], 0.0)), 0.0) * sx3[r]
        hi, mid, lo = split3(w)
        turned = jnp.transpose(
            jnp.concatenate([hi, mid, lo, jnp.broadcast_to(jnp.exp(end), (8, 512))], axis=0)
        )
        b24 = jnp.concatenate([b3[r], b3[r], b3[r]], axis=0).astype(bf16)
        add = jnp.dot(turned[:, 0:24].astype(bf16), b24, preferred_element_type=f32)
        ns_ref[r] = (turned[:, 24:25] * state_v[r].astype(f32) + add).astype(bf16)
    ns_out = pltpu.make_async_copy(ns_ref, ns_hbm, loc_sem.at[15])
    ns_out.start()

    pl.semaphore_wait(past_sem, 2)
    for g in (6, -6):
        embeds_far(g)

    loc_wo.wait()
    c_wo.wait_recv()
    for g in groups:
        i = slot[g]
        n = len(members[g])
        own_inside = functools.reduce(jnp.logical_or, [at(g + d) == 0 for d in members[g]])
        pl.when(own_inside)(lambda n=n, i=i: wait_arrival(g_buf.at[pl.ds(0, n - 1)], ag_r.at[i]))
        pl.when(jnp.logical_not(own_inside))(lambda n=n, i=i: wait_arrival(g_buf.at[pl.ds(0, n)], ag_r.at[i]))
        rows = jnp.concatenate([g_buf[at(g + d)] for d in members[g]], axis=0)
        for h in range(2):
            part = jnp.dot(rows, wo[h], preferred_element_type=f32).reshape(n, 32, 256)
            cols = pl.ds(256 * h, 256)
            p_own[i, :, cols] = part[1]
            p_snd[i, 0:n, :, cols] = part.astype(bf16)
        if g == 6:
            for j in range(2):
                cols = pl.ds(256 * j, 256)
                rc(p_snd.at[0, 3, :, cols], r1.at[j, 2, :, cols], rs_s.at[1 + j], rs_r.at[5 + j], zp(2 - 4 * j))
        rc(p_snd.at[i, 2], r1.at[i, 0], rs_s.at[0], rs_r.at[i], zp(1))
        rc(p_snd.at[i, 0], r1.at[i, 1], rs_s.at[0], rs_r.at[i], zp(-1))

    wait_arrival(ssq_rcv.at[pl.ds(0, 3)], sq_r.at[0])
    window = ssq_own[...] + ssq_rcv[0] + ssq_rcv[1]
    ssq_snd[0] = window
    ssq_snd[1] = window + ssq_rcv[2]
    for i, d in enumerate((3, -3, 6, -6)):
        rc(ssq_snd.at[1 if d == -6 else 0], ssq_rcv.at[3 + i], sq_s.at[1], sq_r.at[1], zp(d))

    for g in groups:
        if g == 0:
            wait_arrival(em.at[pl.ds(0, 4)], ez_r.at[0])
            for e in (6, -6, 3, -3):
                embeds_near(e)
        i = slot[g]
        wait_arrival(r1.at[i, pl.ds(0, 2)], rs_r.at[i])
        p_own[i] = p_own[i] + r1[i, 0].astype(f32) + r1[i, 1].astype(f32)
        if abs(g) == 6:
            cols = pl.ds(0 if g > 0 else 256, 256)
            wait_arrival(r1.at[i, 2, :, cols], rs_r.at[5 if g > 0 else 6])
            p_own[i, :, cols] = p_own[i, :, cols] + r1[i, 2, :, cols].astype(f32)
        if g != 0:
            s_snd[i] = p_own[i].astype(bf16)
            rc(s_snd.at[i], r2.at[i], rf_s.at[0], rf_r.at[i // 2], zp(g))

    wait_arrival(r2.at[pl.ds(2, 2)], rf_r.at[1])
    wait_arrival(r2.at[pl.ds(0, 2)], rf_r.at[0])
    total = p_own[slot[0]]
    for g in (3, -3, 6, -6):
        total = total + r2[slot[g]].astype(f32)
    feat[z] = total.astype(bf16)
    f_far = {}
    for g in (3, -3, 6, -6):
        f_far[g] = rc(feat.at[z], feat.at[z], ff_s.at[0], ff_r.at[slot[g]], zp(g))

    def forward(g):
        c = feat.at[at(-g)]
        if abs(g) == 6:
            h = 0 if g > 0 else 1
            half = feat.at[at(-g), :, pl.ds(256 * h, 256)]
            rc(half, half, fn_s.at[1 + h], fn_r.at[5 + h], zp(2 if g > 0 else -2))
        rc(c, c, fn_s.at[0], fn_r.at[slot[g]], zp(1))
        rc(c, c, fn_s.at[0], fn_r.at[slot[g]], zp(-1))

    forward(0)

    wait_arrival(ssq_rcv.at[pl.ds(3, 4)], sq_r.at[1])
    total = ssq_snd[0] + ssq_rcv[3] + ssq_rcv[4] + ssq_rcv[5] + ssq_rcv[6]
    sc_buf[0] = lax.rsqrt(total / 8192.0 + norm_eps)
    for o in range(1, 16):
        rc(sc_buf.at[0], sc_buf.at[o], sc_s.at[0], sc_r.at[0], xyp(5 * o % 16 // 4, 5 * o % 4))

    loc_wf.wait()
    c_wf.wait_recv()

    def draft_send(o):
        dx, dy = place(o)
        rc(d_snd.at[o], d_rcv.at[o], xr_s.at[0], xr_r.at[0], xyp(-dx, -dy))

    def project(deltas):
        f = jnp.concatenate([feat[at(d)] for d in deltas], axis=0)
        y = jnp.dot(f, wf[...].reshape(512, 512), preferred_element_type=f32)
        for i, d in enumerate(deltas):
            o = at(d)
            scale = jnp.sum(jnp.where(eye, sc_buf[o], 0.0), axis=1, keepdims=True)
            out = y[32 * i : 32 * i + 32] * scale + q_buf[o]
            q_buf[o] = out
            d_snd[o] = out.astype(bf16)
            pl.when(o != 0)(functools.partial(draft_send, o))

    for g in (3, -3):
        i = slot[g]
        f_far[g].wait_recv()
        forward(g)
    wait_arrival(sc_buf.at[pl.ds(1, 15)], sc_r.at[0])
    loc_we.wait()
    c_we.wait_recv()
    wait_arrival(em.at[pl.ds(0, 10)], en_r.at[0])
    wait_arrival(em.at[0, 0], en_r.at[1])
    wait_arrival(em.at[0, 1], en_r.at[2])
    for a in range(4):
        es = []
        for o in range(4 * a, 4 * a + 4):
            dx, dy = 5 * o % 16 // 4, 5 * o % 4
            es.append(em[lax.rem(cx + (4 - dx), 4) * 4 + lax.rem(cy + (4 - dy), 4)])
        q = 0.0
        for h in range(2):
            e = jnp.concatenate([v[h] for v in es], axis=0)
            q = q + jnp.dot(e, we[h], preferred_element_type=f32)
        q_buf[4 * a : 4 * a + 4] = q.reshape(4, 32, 512)
    for g in (6, -6):
        i = slot[g]
        f_far[g].wait_recv()
        forward(g)
    for g, deltas in (
        (0, (-1, 0, 1)), (3, (-4, -3, -2)), (-3, (2, 3, 4)), (6, (-7, -6, -5)), (-6, (5, 6, 7, 8))
    ):
        i = slot[g]
        wait_arrival(feat.at[pl.ds(0, 2)], fn_r.at[i])
        if g == -6:
            wait_arrival(feat.at[0, :, pl.ds(0, 256)], fn_r.at[5])
            wait_arrival(feat.at[0, :, pl.ds(256, 256)], fn_r.at[6])
        project(deltas)

    wait_arrival(d_rcv.at[pl.ds(1, 15)], xr_r.at[0])
    mine = q_buf[0]
    for o in range(1, 16):
        mine = mine + d_rcv[o].astype(f32)
    mine = mine.reshape(4, 8, 512)
    for r in range(4):
        draft_ref[r] = jnp.where(t3[r] <= acc_ref[r], mine[r], 0.0).astype(bf16)
    draft_out = pltpu.make_async_copy(draft_ref, draft_hbm, loc_sem.at[16])
    draft_out.start()
    ns_out.wait()
    for c in (c_em, c_wo, c_we, c_wf):
        c.wait_send()
    chunk_half = feat.at[0, :, pl.ds(0, 256)]
    wait_leave(g_buf.at[pl.ds(1, 15)], ag_s.at[0])
    wait_leave(em.at[pl.ds(0, 4)], ez_s.at[0])
    wait_leave(em.at[pl.ds(0, 10)], en_s.at[0])
    wait_leave(ssq_rcv.at[pl.ds(0, 3)], sq_s.at[0])
    wait_leave(ssq_rcv.at[pl.ds(3, 4)], sq_s.at[1])
    wait_leave(sc_buf.at[pl.ds(1, 15)], sc_s.at[0])
    wait_leave(feat.at[pl.ds(0, 10)], rs_s.at[0])
    wait_leave(r2, rf_s.at[0])
    wait_leave(feat.at[pl.ds(0, 4)], ff_s.at[0])
    wait_leave(feat.at[pl.ds(0, 10)], fn_s.at[0])
    wait_leave(d_rcv.at[pl.ds(1, 15)], xr_s.at[0])
    for sems in (en_s, rs_s, fn_s):
        wait_leave(chunk_half, sems.at[1])
        wait_leave(chunk_half, sems.at[2])
    draft_out.wait()


def finish(draft_in, ns_in, draft_out, ns_out, draft_v, ns_v, sem):
    def moves(i):
        if i == 4:
            return (draft_in, draft_v, sem.at[4]), (draft_v, draft_out, sem.at[9])
        return (ns_in.at[i], ns_v.at[i], sem.at[i]), (ns_v.at[i], ns_out.at[i], sem.at[5 + i])

    arrive = [pltpu.make_async_copy(*moves(i)[0]) for i in range(5)]
    leave = [pltpu.make_async_copy(*moves(i)[1]) for i in range(5)]
    for c in arrive:
        c.start()
    for c, d in zip(arrive, leave):
        c.wait()
        d.start()
    for d in leave:
        d.wait()


def body(
    ssm_input, gate_input, write_vectors, read_vectors, step_logit, step_bias, decay_rate, skip_gain,
    norm_gain, ssm_state, accepted, out_weight, token_embeds, feat_weight, embed_weight,
):
    hbm = pl.BlockSpec(memory_space=pltpu.HBM)
    dma = pltpu.SemaphoreType.DMA
    draft, new_state = pl.pallas_call(
        kernel,
        out_shape=(
            jax.ShapeDtypeStruct((4, 8, 512), bf16),
            jax.ShapeDtypeStruct((4, 512, 256), bf16),
        ),
        in_specs=[hbm] * 15,
        out_specs=(hbm, hbm),
        scratch_shapes=[
            pltpu.VMEM((4, 8, 512), bf16),
            pltpu.VMEM((4, 8, 512), bf16),
            pltpu.VMEM((4, 8, 256), bf16),
            pltpu.VMEM((4, 8, 256), bf16),
            pltpu.VMEM((4, 8, 8), f32),
            pltpu.SMEM((8,), f32),
            pltpu.SMEM((8,), f32),
            pltpu.SMEM((8,), f32),
            pltpu.VMEM((512,), f32),
            pltpu.SMEM((4,), jnp.int32),
            pltpu.VMEM((8, 8, 256), bf16),
            pltpu.VMEM((4, 8, 512), bf16),
            pltpu.VMEM((4, 512, 256), bf16),
            pltpu.VMEM((4, 512, 256), bf16),
            pltpu.VMEM((2, 512, 256), bf16),
            pltpu.VMEM((2, 256, 512), bf16),
            pltpu.VMEM((2, 256, 512), bf16),
            pltpu.VMEM((2, 32, 256), bf16),
            pltpu.VMEM((16, 2, 32, 256), bf16),
            pltpu.VMEM((16, 32, 512), bf16),
            pltpu.VMEM((5, 32, 512), f32),
            pltpu.VMEM((5, 4, 32, 512), bf16),
            pltpu.VMEM((5, 3, 32, 512), bf16),
            pltpu.VMEM((4, 32, 512), bf16),
            pltpu.VMEM((4, 32, 512), bf16),
            pltpu.VMEM((16, 32, 512), bf16),
            pltpu.VMEM((16, 32, 512), f32),
            pltpu.VMEM((16, 32, 512), bf16),
            pltpu.VMEM((16, 32, 512), bf16),
            pltpu.VMEM((1, 128), f32),
            pltpu.VMEM((2, 1, 128), f32),
            pltpu.VMEM((7, 1, 128), f32),
            pltpu.VMEM((16, 1, 128), f32),
            pltpu.SemaphoreType.REGULAR,
            dma((17,)),
            dma((4,)), dma((4,)),
            dma((1,)), dma((1,)),
            dma((3,)), dma((3,)),
            dma((1,)), dma((5,)),
            dma((2,)), dma((2,)),
            dma((1,)), dma((1,)),
            dma((3,)), dma((7,)),
            dma((1,)), dma((2,)),
            dma((1,)), dma((4,)),
            dma((3,)), dma((7,)),
            dma((1,)), dma((1,)),
        ],
        compiler_params=pltpu.CompilerParams(
            collective_id=0, has_side_effects=True, vmem_limit_bytes=56 * 1024 * 1024
        ),
        name="verify_step",
    )(
        ssm_input, gate_input, write_vectors, read_vectors, step_logit, step_bias, decay_rate, skip_gain,
        norm_gain, ssm_state.reshape(4, 512, 256), accepted, out_weight, token_embeds, feat_weight, embed_weight,
    )
    draft, new_state = pl.pallas_call(
        finish,
        out_shape=(
            jax.ShapeDtypeStruct((4, 8, 512), bf16),
            jax.ShapeDtypeStruct((4, 512, 256), bf16),
        ),
        in_specs=[hbm] * 2,
        out_specs=(hbm, hbm),
        scratch_shapes=[pltpu.VMEM((4, 8, 512), bf16), pltpu.VMEM((4, 512, 256), bf16), dma((10,))],
        name="results",
    )(draft, new_state)
    return draft, new_state.reshape(4, 8, 64, 256)


def solution(mesh):
    in_specs = (
        P("row", None, "tensor"),
        P("row", None, "tensor"),
        P("row", None, "tensor"),
        P("row", None, "tensor"),
        P("row", None, "tensor"),
        P("tensor"),
        P("tensor"),
        P("tensor"),
        P("tensor"),
        P("row", "tensor", None, None),
        P("row"),
        P("tensor", "row"),
        P("tensor", None, "row"),
        P("row", "tensor"),
        P("row", "tensor"),
    )
    out_specs = (P("row", None, "tensor"), P("row", "tensor", None, None))
    return jax.shard_map(body, mesh=mesh, in_specs=in_specs, out_specs=out_specs, check_vma=False)
```

```python
import functools

import jax
import jax.numpy as jnp
from jax import lax
from jax.experimental import pallas as pl
from jax.experimental.pallas import tpu as pltpu
from jax.sharding import PartitionSpec as P

norm_eps = 1e-05
MESH = pl.DeviceIdType.MESH
f32 = jnp.float32
bf16 = jnp.bfloat16


def nt_dot(a, b):
    return lax.dot_general(a, b, (((1,), (1,)), ((), ())), preferred_element_type=f32)


def split3(v):
    hi = v.astype(bf16).astype(f32)
    mid = (v - hi).astype(bf16).astype(f32)
    return hi, mid, v - hi - mid


def kernel(
    x_hbm, gate_hbm, b_hbm, c_hbm, logit_hbm, bias_hbm, decay_hbm, skip_hbm, gain_hbm, state_hbm, acc_hbm,
    wo_hbm, emb_hbm, wf_hbm, we_hbm,
    draft_hbm, ns_hbm,
    x_ref, gate_ref, b_ref, c_ref, logit_ref, bias_ref, decay_ref, skip_ref, gain_ref, acc_ref, emb_ref,
    draft_ref, ns_ref, state_v, wo, wf, we, em_own, em, g_buf, p_own, p_snd, r1, s_snd, r2, feat, q_buf, d_snd, d_rcv,
    ssq_own, ssq_snd, ssq_rcv, sc_buf,
    past_sem, loc_sem, sib_s, sib_r, ez_s, ez_r, en_s, en_r, ag_s, ag_r, sq_s, sq_r, sc_s, sc_r, rs_s, rs_r,
    rf_s, rf_r, ff_s, ff_r, fn_s, fn_r, xr_s, xr_r,
):
    groups = (6, -6, 3, -3, 0)
    slot = {g: i for i, g in enumerate(groups)}
    row = lax.axis_index("row")
    z = lax.axis_index("tensor")
    core = lax.rem(row, 2)
    chip = row // 2
    cx = chip // 4
    cy = lax.rem(chip, 4)
    sib = (row + 1 - 2 * core, z)

    def at(d):
        return lax.rem(z + (d + 16), 16)

    def zp(d):
        return (row, at(d))

    def xyp(dx, dy):
        return ((lax.rem(cx + (dx + 4), 4) * 4 + lax.rem(cy + (dy + 4), 4)) * 2 + core, z)

    def place(o):
        p = lax.rem(5 * o, 16)
        return p // 4, lax.rem(p, 4)

    xy_all = [(a, b) for a in range(4) for b in range(4) if (a, b) != (0, 0)]
    barrier = pltpu.get_barrier_semaphore()
    peers = [xyp(a, b) for a, b in sorted(xy_all, key=lambda p: -min(p[0], 4 - p[0]) - min(p[1], 4 - p[1]))]
    peers += [zp(3), zp(-3), (sib[0], at(3)), (sib[0], at(-3)), zp(2), zp(-2), zp(1), zp(-1), sib]
    for p in peers:
        pl.semaphore_signal(barrier, inc=1, device_id=p, device_id_type=MESH)

    def rc(src, dst, ss, rs, dev):
        c = pltpu.make_async_remote_copy(
            src_ref=src, dst_ref=dst, send_sem=ss, recv_sem=rs, device_id=dev, device_id_type=MESH
        )
        c.start()
        return c

    def wait_arrival(ref, sem):
        pltpu.make_async_remote_copy(
            src_ref=ref, dst_ref=ref, send_sem=sem, recv_sem=sem, device_id=sib, device_id_type=MESH
        ).wait_recv()

    def wait_leave(ref, sem):
        pltpu.make_async_remote_copy(
            src_ref=ref, dst_ref=ref, send_sem=sem, recv_sem=sem, device_id=sib, device_id_type=MESH
        ).wait_send()

    loc = []
    for i, (s, d) in enumerate(
        (
            (emb_hbm, emb_ref), (logit_hbm, logit_ref), (bias_hbm, bias_ref), (decay_hbm, decay_ref),
            (skip_hbm, skip_ref), (acc_hbm, acc_ref), (x_hbm, x_ref), (c_hbm, c_ref), (b_hbm, b_ref),
            (gate_hbm, gate_ref), (gain_hbm, gain_ref), (state_hbm, state_v), (wo_hbm, wo.at[0]),
            (we_hbm, we.at[0]), (wf_hbm, wf.at[0]),
        )
    ):
        c = pltpu.make_async_copy(s, d, loc_sem.at[i])
        c.start()
        loc.append(c)
    loc_wo, loc_we, loc_wf = loc[12:]

    loc[0].wait()
    em_own[...] = emb_ref[...].astype(f32).reshape(2, 32, 256).astype(bf16)
    em[z, 0] = em_own[core]

    for c in loc[1:11]:
        c.wait()
    x3 = x_ref[...].astype(f32)
    c3 = c_ref[...].astype(f32)
    b3 = b_ref[...].astype(f32)
    lane_head = lax.broadcasted_iota(jnp.int32, (8, 512), 1) // 64
    pick = (lane_head == lax.broadcasted_iota(jnp.int32, (8, 512), 0)).astype(f32)
    bias = jnp.zeros((1, 8), f32)
    decay_x = jnp.zeros((1, 512), f32)
    skip_x = jnp.zeros((1, 512), f32)
    for h in range(8):
        bias = jnp.where(lax.broadcasted_iota(jnp.int32, (1, 8), 1) == h, bias_ref[h], bias)
        decay_x = jnp.where(lane_head[0:1] == h, decay_ref[h], decay_x)
        skip_x = jnp.where(lane_head[0:1] == h, skip_ref[h], skip_x)

    def expand(v):
        return jnp.dot(v, pick, precision=lax.Precision.HIGHEST, preferred_element_type=f32)

    step = jax.nn.softplus(logit_ref[...].reshape(32, 8) + bias)
    step_x = expand(step)
    log_x = -step_x * decay_x
    t_in = lax.rem(lax.broadcasted_iota(jnp.int32, (32, 512), 0), 8)
    for k in (1, 2, 4):
        log_x = log_x + jnp.where(t_in >= k, pltpu.roll(log_x, k, 0), 0.0)
    log3 = log_x.reshape(4, 8, 512)
    step3 = step_x.reshape(4, 8, 512)
    sx3 = step3 * x3
    t3 = lax.broadcasted_iota(jnp.int32, (4, 8, 512), 1)
    gmat = [nt_dot(c3[r].astype(bf16), b3[r].astype(bf16)) for r in range(4)]
    intra = skip_x * x3
    for s in range(8):
        keep = t3 >= s
        e = jnp.where(keep, jnp.exp(jnp.where(keep, log3 - log3[:, s : s + 1, :], 0.0)), 0.0)
        gcol = jnp.stack([gmat[r][:, s : s + 1] for r in range(4)], axis=0)
        intra = intra + e * gcol * sx3[:, s : s + 1, :]
    loc[11].wait()
    carried = jnp.stack([nt_dot(c3[r].astype(bf16), state_v[r]) for r in range(4)], axis=0)
    mixed = jnp.exp(log3) * carried + intra
    gate = gate_ref[...].astype(f32)
    gated = (mixed * (gate / (1.0 + jnp.exp(-gate)))).reshape(32, 512)
    g_buf[0] = (gated * gain_ref[...].reshape(1, 512)).astype(bf16)
    ssq = jnp.sum(gated * gated, axis=1, keepdims=True)
    eye = lax.broadcasted_iota(jnp.int32, (32, 128), 0) == lax.broadcasted_iota(jnp.int32, (32, 128), 1)
    ssq_own[...] = jnp.sum(jnp.where(eye, ssq, 0.0), axis=0, keepdims=True)

    pl.semaphore_wait(barrier, len(peers))
    def normed_send(o, i):
        dx, dy = place(o)
        rc(g_buf.at[0], g_buf.at[o], ag_s.at[0], ag_r.at[i], xyp(dx, dy))

    members = {g: (-1, 0, 1, 2) if g == 6 else (-1, 0, 1) for g in groups}
    for g in groups:
        for d in members[g]:
            o = at(g + d)
            pl.when(o != 0)(functools.partial(normed_send, o, slot[g]))
    c_em = rc(em_own.at[1 - core], em.at[z, 1], sib_s.at[0], sib_r.at[0], sib)
    c_wo = rc(wo_hbm, wo.at[1], sib_s.at[1], sib_r.at[1], sib)
    c_we = rc(we_hbm, we.at[1], sib_s.at[2], sib_r.at[2], sib)
    c_wf = rc(wf_hbm, wf.at[1], sib_s.at[3], sib_r.at[3], sib)

    def embeds_far(g):
        rc(em_own.at[core], em.at[z, 0], ez_s.at[0], ez_r.at[0], zp(g))
        rc(em_own.at[1 - core], em.at[z, 1], ez_s.at[0], ez_r.at[0], (sib[0], at(g)))

    for g in (3, -3):
        pl.semaphore_signal(past_sem, inc=1, device_id=zp(g), device_id_type=MESH)
        embeds_far(g)

    def embeds_near(g):
        o = at(-g)
        if g == 6:
            rc(em.at[o, 0], em.at[o, 0], en_s.at[1], en_r.at[1], zp(2))
        if g == -6:
            rc(em.at[o, 1], em.at[o, 1], en_s.at[2], en_r.at[2], zp(-2))
        rc(em.at[o], em.at[o], en_s.at[0], en_r.at[0], zp(1))
        rc(em.at[o], em.at[o], en_s.at[0], en_r.at[0], zp(-1))

    for i, d in enumerate((1, -1, -2)):
        rc(ssq_own, ssq_rcv.at[i], sq_s.at[0], sq_r.at[0], zp(d))
    c_em.wait_recv()
    embeds_near(0)

    for r in range(4):
        k = acc_ref[r]
        t2 = t3[r]
        end = jnp.sum(jnp.where(t2 == k - 1, log3[r], 0.0), axis=0, keepdims=True)
        kept = t2 < k
        w = jnp.where(kept, jnp.exp(jnp.where(kept, end - log3[r], 0.0)), 0.0) * sx3[r]
        hi, mid, lo = split3(w)
        turned = jnp.transpose(
            jnp.concatenate([hi, mid, lo, jnp.broadcast_to(jnp.exp(end), (8, 512))], axis=0)
        )
        b24 = jnp.concatenate([b3[r], b3[r], b3[r]], axis=0).astype(bf16)
        add = jnp.dot(turned[:, 0:24].astype(bf16), b24, preferred_element_type=f32)
        ns_ref[r] = (turned[:, 24:25] * state_v[r].astype(f32) + add).astype(bf16)
    ns_out = pltpu.make_async_copy(ns_ref, ns_hbm, loc_sem.at[15])
    ns_out.start()

    pl.semaphore_wait(past_sem, 2)
    for g in (6, -6):
        embeds_far(g)

    loc_wo.wait()
    c_wo.wait_recv()
    for g in groups:
        i = slot[g]
        n = len(members[g])
        own_inside = functools.reduce(jnp.logical_or, [at(g + d) == 0 for d in members[g]])
        pl.when(own_inside)(lambda n=n, i=i: wait_arrival(g_buf.at[pl.ds(0, n - 1)], ag_r.at[i]))
        pl.when(jnp.logical_not(own_inside))(lambda n=n, i=i: wait_arrival(g_buf.at[pl.ds(0, n)], ag_r.at[i]))
        rows = jnp.concatenate([g_buf[at(g + d)] for d in members[g]], axis=0)
        for h in range(2):
            part = jnp.dot(rows, wo[h], preferred_element_type=f32).reshape(n, 32, 256)
            cols = pl.ds(256 * h, 256)
            p_own[i, :, cols] = part[1]
            p_snd[i, 0:n, :, cols] = part.astype(bf16)
        if g == 6:
            for j in range(2):
                cols = pl.ds(256 * j, 256)
                rc(p_snd.at[0, 3, :, cols], r1.at[j, 2, :, cols], rs_s.at[1 + j], rs_r.at[5 + j], zp(2 - 4 * j))
        rc(p_snd.at[i, 2], r1.at[i, 0], rs_s.at[0], rs_r.at[i], zp(1))
        rc(p_snd.at[i, 0], r1.at[i, 1], rs_s.at[0], rs_r.at[i], zp(-1))

    wait_arrival(ssq_rcv.at[pl.ds(0, 3)], sq_r.at[0])
    window = ssq_own[...] + ssq_rcv[0] + ssq_rcv[1]
    ssq_snd[0] = window
    ssq_snd[1] = window + ssq_rcv[2]
    for i, d in enumerate((3, -3, 6, -6)):
        rc(ssq_snd.at[1 if d == -6 else 0], ssq_rcv.at[3 + i], sq_s.at[1], sq_r.at[1], zp(d))

    for g in groups:
        if g == 0:
            wait_arrival(em.at[pl.ds(0, 4)], ez_r.at[0])
            for e in (6, -6, 3, -3):
                embeds_near(e)
        i = slot[g]
        wait_arrival(r1.at[i, pl.ds(0, 2)], rs_r.at[i])
        p_own[i] = p_own[i] + r1[i, 0].astype(f32) + r1[i, 1].astype(f32)
        if abs(g) == 6:
            cols = pl.ds(0 if g > 0 else 256, 256)
            wait_arrival(r1.at[i, 2, :, cols], rs_r.at[5 if g > 0 else 6])
            p_own[i, :, cols] = p_own[i, :, cols] + r1[i, 2, :, cols].astype(f32)
        if g != 0:
            s_snd[i] = p_own[i].astype(bf16)
            rc(s_snd.at[i], r2.at[i], rf_s.at[0], rf_r.at[i // 2], zp(g))

    wait_arrival(r2.at[pl.ds(2, 2)], rf_r.at[1])
    wait_arrival(r2.at[pl.ds(0, 2)], rf_r.at[0])
    total = p_own[slot[0]]
    for g in (3, -3, 6, -6):
        total = total + r2[slot[g]].astype(f32)
    feat[z] = total.astype(bf16)
    f_far = {}
    for g in (6, -6, 3, -3):
        f_far[g] = rc(feat.at[z], feat.at[z], ff_s.at[0], ff_r.at[slot[g]], zp(g))

    def forward(g):
        c = feat.at[at(-g)]
        if abs(g) == 6:
            h = 0 if g > 0 else 1
            half = feat.at[at(-g), :, pl.ds(256 * h, 256)]
            rc(half, half, fn_s.at[1 + h], fn_r.at[5 + h], zp(2 if g > 0 else -2))
        rc(c, c, fn_s.at[0], fn_r.at[slot[g]], zp(1))
        rc(c, c, fn_s.at[0], fn_r.at[slot[g]], zp(-1))

    forward(0)

    wait_arrival(ssq_rcv.at[pl.ds(3, 4)], sq_r.at[1])
    total = ssq_snd[0] + ssq_rcv[3] + ssq_rcv[4] + ssq_rcv[5] + ssq_rcv[6]
    sc_buf[0] = lax.rsqrt(total / 8192.0 + norm_eps)
    for o in range(1, 16):
        rc(sc_buf.at[0], sc_buf.at[o], sc_s.at[0], sc_r.at[0], xyp(5 * o % 16 // 4, 5 * o % 4))

    loc_wf.wait()
    c_wf.wait_recv()

    def draft_send(o):
        dx, dy = place(o)
        rc(d_snd.at[o], d_rcv.at[o], xr_s.at[0], xr_r.at[0], xyp(-dx, -dy))

    def project(deltas):
        f = jnp.concatenate([feat[at(d)] for d in deltas], axis=0)
        y = jnp.dot(f, wf[...].reshape(512, 512), preferred_element_type=f32)
        for i, d in enumerate(deltas):
            o = at(d)
            scale = jnp.sum(jnp.where(eye, sc_buf[o], 0.0), axis=1, keepdims=True)
            out = y[32 * i : 32 * i + 32] * scale + q_buf[o]
            q_buf[o] = out
            d_snd[o] = out.astype(bf16)
            pl.when(o != 0)(functools.partial(draft_send, o))

    for g in (3, -3):
        i = slot[g]
        f_far[g].wait_recv()
        forward(g)
    wait_arrival(sc_buf.at[pl.ds(1, 15)], sc_r.at[0])
    loc_we.wait()
    c_we.wait_recv()
    wait_arrival(em.at[pl.ds(0, 10)], en_r.at[0])
    wait_arrival(em.at[0, 0], en_r.at[1])
    wait_arrival(em.at[0, 1], en_r.at[2])
    for a in range(4):
        es = []
        for o in range(4 * a, 4 * a + 4):
            dx, dy = 5 * o % 16 // 4, 5 * o % 4
            es.append(em[lax.rem(cx + (4 - dx), 4) * 4 + lax.rem(cy + (4 - dy), 4)])
        q = 0.0
        for h in range(2):
            e = jnp.concatenate([v[h] for v in es], axis=0)
            q = q + jnp.dot(e, we[h], preferred_element_type=f32)
        q_buf[4 * a : 4 * a + 4] = q.reshape(4, 32, 512)
    for g in (6, -6):
        i = slot[g]
        f_far[g].wait_recv()
        forward(g)
    for g, deltas in (
        (0, (-1, 0, 1)), (3, (-4, -3, -2)), (-3, (2, 3, 4)), (6, (-7, -6, -5)), (-6, (5, 6, 7, 8))
    ):
        i = slot[g]
        wait_arrival(feat.at[pl.ds(0, 2)], fn_r.at[i])
        if g == -6:
            wait_arrival(feat.at[0, :, pl.ds(0, 256)], fn_r.at[5])
            wait_arrival(feat.at[0, :, pl.ds(256, 256)], fn_r.at[6])
        project(deltas)

    wait_arrival(d_rcv.at[pl.ds(1, 15)], xr_r.at[0])
    mine = q_buf[0]
    for o in range(1, 16):
        mine = mine + d_rcv[o].astype(f32)
    mine = mine.reshape(4, 8, 512)
    for r in range(4):
        draft_ref[r] = jnp.where(t3[r] <= acc_ref[r], mine[r], 0.0).astype(bf16)
    draft_out = pltpu.make_async_copy(draft_ref, draft_hbm, loc_sem.at[16])
    draft_out.start()
    ns_out.wait()
    for c in (c_em, c_wo, c_we, c_wf):
        c.wait_send()
    chunk_half = feat.at[0, :, pl.ds(0, 256)]
    wait_leave(g_buf.at[pl.ds(1, 15)], ag_s.at[0])
    wait_leave(em.at[pl.ds(0, 4)], ez_s.at[0])
    wait_leave(em.at[pl.ds(0, 10)], en_s.at[0])
    wait_leave(ssq_rcv.at[pl.ds(0, 3)], sq_s.at[0])
    wait_leave(ssq_rcv.at[pl.ds(3, 4)], sq_s.at[1])
    wait_leave(sc_buf.at[pl.ds(1, 15)], sc_s.at[0])
    wait_leave(feat.at[pl.ds(0, 10)], rs_s.at[0])
    wait_leave(r2, rf_s.at[0])
    wait_leave(feat.at[pl.ds(0, 4)], ff_s.at[0])
    wait_leave(feat.at[pl.ds(0, 10)], fn_s.at[0])
    wait_leave(d_rcv.at[pl.ds(1, 15)], xr_s.at[0])
    for sems in (en_s, rs_s, fn_s):
        wait_leave(chunk_half, sems.at[1])
        wait_leave(chunk_half, sems.at[2])
    draft_out.wait()


def finish(draft_in, ns_in, draft_out, ns_out, draft_v, ns_v, sem):
    def moves(i):
        if i == 4:
            return (draft_in, draft_v, sem.at[4]), (draft_v, draft_out, sem.at[9])
        return (ns_in.at[i], ns_v.at[i], sem.at[i]), (ns_v.at[i], ns_out.at[i], sem.at[5 + i])

    arrive = [pltpu.make_async_copy(*moves(i)[0]) for i in range(5)]
    leave = [pltpu.make_async_copy(*moves(i)[1]) for i in range(5)]
    for c in arrive:
        c.start()
    for c, d in zip(arrive, leave):
        c.wait()
        d.start()
    for d in leave:
        d.wait()


def body(
    ssm_input, gate_input, write_vectors, read_vectors, step_logit, step_bias, decay_rate, skip_gain,
    norm_gain, ssm_state, accepted, out_weight, token_embeds, feat_weight, embed_weight,
):
    hbm = pl.BlockSpec(memory_space=pltpu.HBM)
    dma = pltpu.SemaphoreType.DMA
    draft, new_state = pl.pallas_call(
        kernel,
        out_shape=(
            jax.ShapeDtypeStruct((4, 8, 512), bf16),
            jax.ShapeDtypeStruct((4, 512, 256), bf16),
        ),
        in_specs=[hbm] * 15,
        out_specs=(hbm, hbm),
        scratch_shapes=[
            pltpu.VMEM((4, 8, 512), bf16),
            pltpu.VMEM((4, 8, 512), bf16),
            pltpu.VMEM((4, 8, 256), bf16),
            pltpu.VMEM((4, 8, 256), bf16),
            pltpu.VMEM((4, 8, 8), f32),
            pltpu.SMEM((8,), f32),
            pltpu.SMEM((8,), f32),
            pltpu.SMEM((8,), f32),
            pltpu.VMEM((512,), f32),
            pltpu.SMEM((4,), jnp.int32),
            pltpu.VMEM((8, 8, 256), bf16),
            pltpu.VMEM((4, 8, 512), bf16),
            pltpu.VMEM((4, 512, 256), bf16),
            pltpu.VMEM((4, 512, 256), bf16),
            pltpu.VMEM((2, 512, 256), bf16),
            pltpu.VMEM((2, 256, 512), bf16),
            pltpu.VMEM((2, 256, 512), bf16),
            pltpu.VMEM((2, 32, 256), bf16),
            pltpu.VMEM((16, 2, 32, 256), bf16),
            pltpu.VMEM((16, 32, 512), bf16),
            pltpu.VMEM((5, 32, 512), f32),
            pltpu.VMEM((5, 4, 32, 512), bf16),
            pltpu.VMEM((5, 3, 32, 512), bf16),
            pltpu.VMEM((4, 32, 512), bf16),
            pltpu.VMEM((4, 32, 512), bf16),
            pltpu.VMEM((16, 32, 512), bf16),
            pltpu.VMEM((16, 32, 512), f32),
            pltpu.VMEM((16, 32, 512), bf16),
            pltpu.VMEM((16, 32, 512), bf16),
            pltpu.VMEM((1, 128), f32),
            pltpu.VMEM((2, 1, 128), f32),
            pltpu.VMEM((7, 1, 128), f32),
            pltpu.VMEM((16, 1, 128), f32),
            pltpu.SemaphoreType.REGULAR,
            dma((17,)),
            dma((4,)), dma((4,)),
            dma((1,)), dma((1,)),
            dma((3,)), dma((3,)),
            dma((1,)), dma((5,)),
            dma((2,)), dma((2,)),
            dma((1,)), dma((1,)),
            dma((3,)), dma((7,)),
            dma((1,)), dma((2,)),
            dma((1,)), dma((4,)),
            dma((3,)), dma((7,)),
            dma((1,)), dma((1,)),
        ],
        compiler_params=pltpu.CompilerParams(
            collective_id=0, has_side_effects=True, vmem_limit_bytes=56 * 1024 * 1024
        ),
        name="verify_step",
    )(
        ssm_input, gate_input, write_vectors, read_vectors, step_logit, step_bias, decay_rate, skip_gain,
        norm_gain, ssm_state.reshape(4, 512, 256), accepted, out_weight, token_embeds, feat_weight, embed_weight,
    )
    draft, new_state = pl.pallas_call(
        finish,
        out_shape=(
            jax.ShapeDtypeStruct((4, 8, 512), bf16),
            jax.ShapeDtypeStruct((4, 512, 256), bf16),
        ),
        in_specs=[hbm] * 2,
        out_specs=(hbm, hbm),
        scratch_shapes=[pltpu.VMEM((4, 8, 512), bf16), pltpu.VMEM((4, 512, 256), bf16), dma((10,))],
        name="results",
    )(draft, new_state)
    return draft, new_state.reshape(4, 8, 64, 256)


def solution(mesh):
    in_specs = (
        P("row", None, "tensor"),
        P("row", None, "tensor"),
        P("row", None, "tensor"),
        P("row", None, "tensor"),
        P("row", None, "tensor"),
        P("tensor"),
        P("tensor"),
        P("tensor"),
        P("tensor"),
        P("row", "tensor", None, None),
        P("row"),
        P("tensor", "row"),
        P("tensor", None, "row"),
        P("row", "tensor"),
        P("row", "tensor"),
    )
    out_specs = (P("row", None, "tensor"), P("row", "tensor", None, None))
    return jax.shard_map(body, mesh=mesh, in_specs=in_specs, out_specs=out_specs, check_vma=False)
```

```python
import functools

import jax
import jax.numpy as jnp
from jax import lax
from jax.experimental import pallas as pl
from jax.experimental.pallas import tpu as pltpu
from jax.sharding import PartitionSpec as P

norm_eps = 1e-05
MESH = pl.DeviceIdType.MESH
f32 = jnp.float32
bf16 = jnp.bfloat16


def nt_dot(a, b):
    return lax.dot_general(a, b, (((1,), (1,)), ((), ())), preferred_element_type=f32)


def split3(v):
    hi = v.astype(bf16).astype(f32)
    mid = (v - hi).astype(bf16).astype(f32)
    return hi, mid, v - hi - mid


def kernel(
    x_hbm, gate_hbm, b_hbm, c_hbm, logit_hbm, bias_hbm, decay_hbm, skip_hbm, gain_hbm, state_hbm, acc_hbm,
    wo_hbm, emb_hbm, wf_hbm, we_hbm,
    draft_hbm, ns_hbm,
    x_ref, gate_ref, b_ref, c_ref, logit_ref, bias_ref, decay_ref, skip_ref, gain_ref, acc_ref, emb_ref,
    draft_ref, ns_ref, state_v, wo, wf, we, em_own, em, g_buf, p_own, p_snd, r1, s_snd, r2, feat, q_buf, d_snd, d_rcv,
    ssq_own, ssq_snd, ssq_rcv, sc_buf,
    past_sem, loc_sem, sib_s, sib_r, ez_s, ez_r, en_s, en_r, ag_s, ag_r, sq_s, sq_r, sc_s, sc_r, rs_s, rs_r,
    rf_s, rf_r, ff_s, ff_r, fn_s, fn_r, xr_s, xr_r,
):
    groups = (6, -6, 3, -3, 0)
    slot = {g: i for i, g in enumerate(groups)}
    row = lax.axis_index("row")
    z = lax.axis_index("tensor")
    core = lax.rem(row, 2)
    chip = row // 2
    cx = chip // 4
    cy = lax.rem(chip, 4)
    sib = (row + 1 - 2 * core, z)

    def at(d):
        return lax.rem(z + (d + 16), 16)

    def zp(d):
        return (row, at(d))

    def xyp(dx, dy):
        return ((lax.rem(cx + (dx + 4), 4) * 4 + lax.rem(cy + (dy + 4), 4)) * 2 + core, z)

    def place(o):
        p = lax.rem(5 * o, 16)
        return p // 4, lax.rem(p, 4)

    xy_all = [(a, b) for a in range(4) for b in range(4) if (a, b) != (0, 0)]
    barrier = pltpu.get_barrier_semaphore()
    peers = [xyp(a, b) for a, b in sorted(xy_all, key=lambda p: -min(p[0], 4 - p[0]) - min(p[1], 4 - p[1]))]
    peers += [zp(3), zp(-3), (sib[0], at(3)), (sib[0], at(-3)), zp(2), zp(-2), zp(1), zp(-1), sib]
    for p in peers:
        pl.semaphore_signal(barrier, inc=1, device_id=p, device_id_type=MESH)

    def rc(src, dst, ss, rs, dev):
        c = pltpu.make_async_remote_copy(
            src_ref=src, dst_ref=dst, send_sem=ss, recv_sem=rs, device_id=dev, device_id_type=MESH
        )
        c.start()
        return c

    def wait_arrival(ref, sem):
        pltpu.make_async_remote_copy(
            src_ref=ref, dst_ref=ref, send_sem=sem, recv_sem=sem, device_id=sib, device_id_type=MESH
        ).wait_recv()

    def wait_leave(ref, sem):
        pltpu.make_async_remote_copy(
            src_ref=ref, dst_ref=ref, send_sem=sem, recv_sem=sem, device_id=sib, device_id_type=MESH
        ).wait_send()

    loc = []
    for i, (s, d) in enumerate(
        (
            (emb_hbm, emb_ref), (logit_hbm, logit_ref), (bias_hbm, bias_ref), (decay_hbm, decay_ref),
            (skip_hbm, skip_ref), (acc_hbm, acc_ref), (x_hbm, x_ref), (c_hbm, c_ref), (b_hbm, b_ref),
            (gate_hbm, gate_ref), (gain_hbm, gain_ref), (state_hbm, state_v), (wo_hbm, wo.at[0]),
            (we_hbm, we.at[0]), (wf_hbm, wf.at[0]),
        )
    ):
        c = pltpu.make_async_copy(s, d, loc_sem.at[i])
        c.start()
        loc.append(c)
    loc_wo, loc_we, loc_wf = loc[12:]

    loc[0].wait()
    em_own[...] = emb_ref[...].astype(f32).reshape(2, 32, 256).astype(bf16)
    em[z, 0] = em_own[core]

    for c in loc[1:11]:
        c.wait()
    x3 = x_ref[...].astype(f32)
    c3 = c_ref[...].astype(f32)
    b3 = b_ref[...].astype(f32)
    lane_head = lax.broadcasted_iota(jnp.int32, (8, 512), 1) // 64
    pick = (lane_head == lax.broadcasted_iota(jnp.int32, (8, 512), 0)).astype(f32)
    bias = jnp.zeros((1, 8), f32)
    decay_x = jnp.zeros((1, 512), f32)
    skip_x = jnp.zeros((1, 512), f32)
    for h in range(8):
        bias = jnp.where(lax.broadcasted_iota(jnp.int32, (1, 8), 1) == h, bias_ref[h], bias)
        decay_x = jnp.where(lane_head[0:1] == h, decay_ref[h], decay_x)
        skip_x = jnp.where(lane_head[0:1] == h, skip_ref[h], skip_x)

    def expand(v):
        return jnp.dot(v, pick, precision=lax.Precision.HIGHEST, preferred_element_type=f32)

    step = jax.nn.softplus(logit_ref[...].reshape(32, 8) + bias)
    step_x = expand(step)
    log_x = -step_x * decay_x
    t_in = lax.rem(lax.broadcasted_iota(jnp.int32, (32, 512), 0), 8)
    for k in (1, 2, 4):
        log_x = log_x + jnp.where(t_in >= k, pltpu.roll(log_x, k, 0), 0.0)
    log3 = log_x.reshape(4, 8, 512)
    step3 = step_x.reshape(4, 8, 512)
    sx3 = step3 * x3
    t3 = lax.broadcasted_iota(jnp.int32, (4, 8, 512), 1)
    gmat = [nt_dot(c3[r].astype(bf16), b3[r].astype(bf16)) for r in range(4)]
    intra = skip_x * x3
    for s in range(8):
        keep = t3 >= s
        e = jnp.where(keep, jnp.exp(jnp.where(keep, log3 - log3[:, s : s + 1, :], 0.0)), 0.0)
        gcol = jnp.stack([gmat[r][:, s : s + 1] for r in range(4)], axis=0)
        intra = intra + e * gcol * sx3[:, s : s + 1, :]
    loc[11].wait()
    carried = jnp.stack([nt_dot(c3[r].astype(bf16), state_v[r]) for r in range(4)], axis=0)
    mixed = jnp.exp(log3) * carried + intra
    gate = gate_ref[...].astype(f32)
    gated = (mixed * (gate / (1.0 + jnp.exp(-gate)))).reshape(32, 512)
    g_buf[0] = (gated * gain_ref[...].reshape(1, 512)).astype(bf16)
    ssq = jnp.sum(gated * gated, axis=1, keepdims=True)
    eye = lax.broadcasted_iota(jnp.int32, (32, 128), 0) == lax.broadcasted_iota(jnp.int32, (32, 128), 1)
    ssq_own[...] = jnp.sum(jnp.where(eye, ssq, 0.0), axis=0, keepdims=True)

    pl.semaphore_wait(barrier, len(peers))
    def normed_send(o, i):
        dx, dy = place(o)
        rc(g_buf.at[0], g_buf.at[o], ag_s.at[0], ag_r.at[i], xyp(dx, dy))

    members = {g: (-1, 0, 1, 2) if g == 6 else (-1, 0, 1) for g in groups}
    for g in groups:
        for d in members[g]:
            o = at(g + d)
            pl.when(o != 0)(functools.partial(normed_send, o, slot[g]))
    c_em = rc(em_own.at[1 - core], em.at[z, 1], sib_s.at[0], sib_r.at[0], sib)
    c_wo = rc(wo_hbm, wo.at[1], sib_s.at[1], sib_r.at[1], sib)
    c_we = rc(we_hbm, we.at[1], sib_s.at[2], sib_r.at[2], sib)
    c_wf = rc(wf_hbm, wf.at[1], sib_s.at[3], sib_r.at[3], sib)

    def embeds_far(g):
        rc(em_own.at[core], em.at[z, 0], ez_s.at[0], ez_r.at[0], zp(g))
        rc(em_own.at[1 - core], em.at[z, 1], ez_s.at[0], ez_r.at[0], (sib[0], at(g)))

    for g in (3, -3):
        pl.semaphore_signal(past_sem, inc=1, device_id=zp(g), device_id_type=MESH)
        embeds_far(g)

    def embeds_near(g):
        o = at(-g)
        if g == 6:
            rc(em.at[o, 0], em.at[o, 0], en_s.at[1], en_r.at[1], zp(2))
        if g == -6:
            rc(em.at[o, 1], em.at[o, 1], en_s.at[2], en_r.at[2], zp(-2))
        rc(em.at[o], em.at[o], en_s.at[0], en_r.at[0], zp(1))
        rc(em.at[o], em.at[o], en_s.at[0], en_r.at[0], zp(-1))

    for i, d in enumerate((1, -1, -2)):
        rc(ssq_own, ssq_rcv.at[i], sq_s.at[0], sq_r.at[0], zp(d))
    c_em.wait_recv()
    embeds_near(0)

    for r in range(4):
        k = acc_ref[r]
        t2 = t3[r]
        end = jnp.sum(jnp.where(t2 == k - 1, log3[r], 0.0), axis=0, keepdims=True)
        kept = t2 < k
        w = jnp.where(kept, jnp.exp(jnp.where(kept, end - log3[r], 0.0)), 0.0) * sx3[r]
        hi, mid, lo = split3(w)
        turned = jnp.transpose(
            jnp.concatenate([hi, mid, lo, jnp.broadcast_to(jnp.exp(end), (8, 512))], axis=0)
        )
        b24 = jnp.concatenate([b3[r], b3[r], b3[r]], axis=0).astype(bf16)
        add = jnp.dot(turned[:, 0:24].astype(bf16), b24, preferred_element_type=f32)
        ns_ref[r] = (turned[:, 24:25] * state_v[r].astype(f32) + add).astype(bf16)
    ns_out = pltpu.make_async_copy(ns_ref, ns_hbm, loc_sem.at[15])
    ns_out.start()

    pl.semaphore_wait(past_sem, 2)
    for g in (6, -6):
        embeds_far(g)

    loc_wo.wait()
    c_wo.wait_recv()
    for g in groups:
        i = slot[g]
        n = len(members[g])
        own_inside = functools.reduce(jnp.logical_or, [at(g + d) == 0 for d in members[g]])
        pl.when(own_inside)(lambda n=n, i=i: wait_arrival(g_buf.at[pl.ds(0, n - 1)], ag_r.at[i]))
        pl.when(jnp.logical_not(own_inside))(lambda n=n, i=i: wait_arrival(g_buf.at[pl.ds(0, n)], ag_r.at[i]))
        rows = jnp.concatenate([g_buf[at(g + d)] for d in members[g]], axis=0)
        for h in range(2):
            part = jnp.dot(rows, wo[h], preferred_element_type=f32).reshape(n, 32, 256)
            cols = pl.ds(256 * h, 256)
            p_own[i, :, cols] = part[1]
            p_snd[i, 0:n, :, cols] = part.astype(bf16)
        if g == 6:
            for j in range(2):
                cols = pl.ds(256 * j, 256)
                rc(p_snd.at[0, 3, :, cols], r1.at[j, 2, :, cols], rs_s.at[1 + j], rs_r.at[5 + j], zp(2 - 4 * j))
        rc(p_snd.at[i, 2], r1.at[i, 0], rs_s.at[0], rs_r.at[i], zp(1))
        rc(p_snd.at[i, 0], r1.at[i, 1], rs_s.at[0], rs_r.at[i], zp(-1))

    wait_arrival(ssq_rcv.at[pl.ds(0, 3)], sq_r.at[0])
    window = ssq_own[...] + ssq_rcv[0] + ssq_rcv[1]
    ssq_snd[0] = window
    ssq_snd[1] = window + ssq_rcv[2]
    for i, d in enumerate((3, -3, 6, -6)):
        rc(ssq_snd.at[1 if d == -6 else 0], ssq_rcv.at[3 + i], sq_s.at[1], sq_r.at[1], zp(d))

    for g in groups:
        if g == 0:
            wait_arrival(em.at[pl.ds(0, 4)], ez_r.at[0])
            for e in (6, -6, 3, -3):
                embeds_near(e)
        i = slot[g]
        wait_arrival(r1.at[i, pl.ds(0, 2)], rs_r.at[i])
        p_own[i] = p_own[i] + r1[i, 0].astype(f32) + r1[i, 1].astype(f32)
        if abs(g) == 6:
            cols = pl.ds(0 if g > 0 else 256, 256)
            wait_arrival(r1.at[i, 2, :, cols], rs_r.at[5 if g > 0 else 6])
            p_own[i, :, cols] = p_own[i, :, cols] + r1[i, 2, :, cols].astype(f32)
        if g != 0:
            s_snd[i] = p_own[i].astype(bf16)
            rc(s_snd.at[i], r2.at[i], rf_s.at[0], rf_r.at[i // 2], zp(g))

    wait_arrival(r2.at[pl.ds(2, 2)], rf_r.at[1])
    wait_arrival(r2.at[pl.ds(0, 2)], rf_r.at[0])
    total = p_own[slot[0]]
    for g in (3, -3, 6, -6):
        total = total + r2[slot[g]].astype(f32)
    feat[z] = total.astype(bf16)
    f_far = {}
    for g in (6, -6, 3, -3):
        f_far[g] = rc(feat.at[z], feat.at[z], ff_s.at[0], ff_r.at[slot[g]], zp(g))

    def forward(g):
        c = feat.at[at(-g)]
        if abs(g) == 6:
            h = 0 if g > 0 else 1
            half = feat.at[at(-g), :, pl.ds(256 * h, 256)]
            rc(half, half, fn_s.at[1 + h], fn_r.at[5 + h], zp(2 if g > 0 else -2))
        rc(c, c, fn_s.at[0], fn_r.at[slot[g]], zp(1))
        rc(c, c, fn_s.at[0], fn_r.at[slot[g]], zp(-1))

    forward(0)

    wait_arrival(ssq_rcv.at[pl.ds(3, 4)], sq_r.at[1])
    total = ssq_snd[0] + ssq_rcv[3] + ssq_rcv[4] + ssq_rcv[5] + ssq_rcv[6]
    sc_buf[0] = lax.rsqrt(total / 8192.0 + norm_eps)
    for o in range(1, 16):
        rc(sc_buf.at[0], sc_buf.at[o], sc_s.at[0], sc_r.at[0], xyp(5 * o % 16 // 4, 5 * o % 4))

    loc_wf.wait()
    c_wf.wait_recv()

    def draft_send(o, part):
        dx, dy = place(o)
        rc(d_snd.at[o], d_rcv.at[o], xr_s.at[0], xr_r.at[part], xyp(-dx, -dy))

    d_rcv[0] = jnp.zeros((32, 512), bf16)

    def project(deltas, part):
        f = jnp.concatenate([feat[at(d)] for d in deltas], axis=0)
        y = jnp.dot(f, wf[...].reshape(512, 512), preferred_element_type=f32)
        for i, d in enumerate(deltas):
            o = at(d)
            scale = jnp.sum(jnp.where(eye, sc_buf[o], 0.0), axis=1, keepdims=True)
            out = y[32 * i : 32 * i + 32] * scale + q_buf[o]
            q_buf[o] = out
            d_snd[o] = out.astype(bf16)
            pl.when(o != 0)(functools.partial(draft_send, o, part))

    for g in (3, -3):
        i = slot[g]
        f_far[g].wait_recv()
        forward(g)
    wait_arrival(sc_buf.at[pl.ds(1, 15)], sc_r.at[0])
    loc_we.wait()
    c_we.wait_recv()
    wait_arrival(em.at[pl.ds(0, 10)], en_r.at[0])
    wait_arrival(em.at[0, 0], en_r.at[1])
    wait_arrival(em.at[0, 1], en_r.at[2])
    for a in range(4):
        es = []
        for o in range(4 * a, 4 * a + 4):
            dx, dy = 5 * o % 16 // 4, 5 * o % 4
            es.append(em[lax.rem(cx + (4 - dx), 4) * 4 + lax.rem(cy + (4 - dy), 4)])
        q = 0.0
        for h in range(2):
            e = jnp.concatenate([v[h] for v in es], axis=0)
            q = q + jnp.dot(e, we[h], preferred_element_type=f32)
        q_buf[4 * a : 4 * a + 4] = q.reshape(4, 32, 512)
    for g in (6, -6):
        i = slot[g]
        f_far[g].wait_recv()
        forward(g)
    for g, deltas in (
        (0, (-1, 0, 1)), (3, (-4, -3, -2)), (-3, (2, 3, 4)), (6, (-7, -6, -5)), (-6, (5, 6, 7, 8))
    ):
        i = slot[g]
        wait_arrival(feat.at[pl.ds(0, 2)], fn_r.at[i])
        if g == -6:
            wait_arrival(feat.at[0, :, pl.ds(0, 256)], fn_r.at[5])
            wait_arrival(feat.at[0, :, pl.ds(256, 256)], fn_r.at[6])
        project(deltas, 1 if abs(g) == 6 else 0)

    parts = ((0, -1, 1, -2, 2, -3, 3, -4, 4), (5, 6, 7, 8, -5, -6, -7))
    mine = 0.0
    for j, deltas in enumerate(parts):
        n = len(deltas)
        own_inside = functools.reduce(jnp.logical_or, [at(d) == 0 for d in deltas])
        pl.when(own_inside)(lambda n=n, j=j: wait_arrival(d_rcv.at[pl.ds(1, n - 1)], xr_r.at[j]))
        pl.when(jnp.logical_not(own_inside))(lambda n=n, j=j: wait_arrival(d_rcv.at[pl.ds(1, n)], xr_r.at[j]))
        for d in deltas:
            mine = mine + d_rcv[at(d)].astype(f32)
    mine = mine + q_buf[0]
    mine = mine.reshape(4, 8, 512)
    for r in range(4):
        draft_ref[r] = jnp.where(t3[r] <= acc_ref[r], mine[r], 0.0).astype(bf16)
    draft_out = pltpu.make_async_copy(draft_ref, draft_hbm, loc_sem.at[16])
    draft_out.start()
    ns_out.wait()
    for c in (c_em, c_wo, c_we, c_wf):
        c.wait_send()
    chunk_half = feat.at[0, :, pl.ds(0, 256)]
    wait_leave(g_buf.at[pl.ds(1, 15)], ag_s.at[0])
    wait_leave(em.at[pl.ds(0, 4)], ez_s.at[0])
    wait_leave(em.at[pl.ds(0, 10)], en_s.at[0])
    wait_leave(ssq_rcv.at[pl.ds(0, 3)], sq_s.at[0])
    wait_leave(ssq_rcv.at[pl.ds(3, 4)], sq_s.at[1])
    wait_leave(sc_buf.at[pl.ds(1, 15)], sc_s.at[0])
    wait_leave(feat.at[pl.ds(0, 10)], rs_s.at[0])
    wait_leave(r2, rf_s.at[0])
    wait_leave(feat.at[pl.ds(0, 4)], ff_s.at[0])
    wait_leave(feat.at[pl.ds(0, 10)], fn_s.at[0])
    wait_leave(d_rcv.at[pl.ds(1, 15)], xr_s.at[0])
    for sems in (en_s, rs_s, fn_s):
        wait_leave(chunk_half, sems.at[1])
        wait_leave(chunk_half, sems.at[2])
    draft_out.wait()


def finish(draft_in, ns_in, draft_out, ns_out, draft_v, ns_v, sem):
    def moves(i):
        if i == 4:
            return (draft_in, draft_v, sem.at[4]), (draft_v, draft_out, sem.at[9])
        return (ns_in.at[i], ns_v.at[i], sem.at[i]), (ns_v.at[i], ns_out.at[i], sem.at[5 + i])

    arrive = [pltpu.make_async_copy(*moves(i)[0]) for i in range(5)]
    leave = [pltpu.make_async_copy(*moves(i)[1]) for i in range(5)]
    for c in arrive:
        c.start()
    for c, d in zip(arrive, leave):
        c.wait()
        d.start()
    for d in leave:
        d.wait()


def body(
    ssm_input, gate_input, write_vectors, read_vectors, step_logit, step_bias, decay_rate, skip_gain,
    norm_gain, ssm_state, accepted, out_weight, token_embeds, feat_weight, embed_weight,
):
    hbm = pl.BlockSpec(memory_space=pltpu.HBM)
    dma = pltpu.SemaphoreType.DMA
    draft, new_state = pl.pallas_call(
        kernel,
        out_shape=(
            jax.ShapeDtypeStruct((4, 8, 512), bf16),
            jax.ShapeDtypeStruct((4, 512, 256), bf16),
        ),
        in_specs=[hbm] * 15,
        out_specs=(hbm, hbm),
        scratch_shapes=[
            pltpu.VMEM((4, 8, 512), bf16),
            pltpu.VMEM((4, 8, 512), bf16),
            pltpu.VMEM((4, 8, 256), bf16),
            pltpu.VMEM((4, 8, 256), bf16),
            pltpu.VMEM((4, 8, 8), f32),
            pltpu.SMEM((8,), f32),
            pltpu.SMEM((8,), f32),
            pltpu.SMEM((8,), f32),
            pltpu.VMEM((512,), f32),
            pltpu.SMEM((4,), jnp.int32),
            pltpu.VMEM((8, 8, 256), bf16),
            pltpu.VMEM((4, 8, 512), bf16),
            pltpu.VMEM((4, 512, 256), bf16),
            pltpu.VMEM((4, 512, 256), bf16),
            pltpu.VMEM((2, 512, 256), bf16),
            pltpu.VMEM((2, 256, 512), bf16),
            pltpu.VMEM((2, 256, 512), bf16),
            pltpu.VMEM((2, 32, 256), bf16),
            pltpu.VMEM((16, 2, 32, 256), bf16),
            pltpu.VMEM((16, 32, 512), bf16),
            pltpu.VMEM((5, 32, 512), f32),
            pltpu.VMEM((5, 4, 32, 512), bf16),
            pltpu.VMEM((5, 3, 32, 512), bf16),
            pltpu.VMEM((4, 32, 512), bf16),
            pltpu.VMEM((4, 32, 512), bf16),
            pltpu.VMEM((16, 32, 512), bf16),
            pltpu.VMEM((16, 32, 512), f32),
            pltpu.VMEM((16, 32, 512), bf16),
            pltpu.VMEM((16, 32, 512), bf16),
            pltpu.VMEM((1, 128), f32),
            pltpu.VMEM((2, 1, 128), f32),
            pltpu.VMEM((7, 1, 128), f32),
            pltpu.VMEM((16, 1, 128), f32),
            pltpu.SemaphoreType.REGULAR,
            dma((17,)),
            dma((4,)), dma((4,)),
            dma((1,)), dma((1,)),
            dma((3,)), dma((3,)),
            dma((1,)), dma((5,)),
            dma((2,)), dma((2,)),
            dma((1,)), dma((1,)),
            dma((3,)), dma((7,)),
            dma((1,)), dma((2,)),
            dma((1,)), dma((4,)),
            dma((3,)), dma((7,)),
            dma((1,)), dma((2,)),
        ],
        compiler_params=pltpu.CompilerParams(
            collective_id=0, has_side_effects=True, vmem_limit_bytes=56 * 1024 * 1024
        ),
        name="verify_step",
    )(
        ssm_input, gate_input, write_vectors, read_vectors, step_logit, step_bias, decay_rate, skip_gain,
        norm_gain, ssm_state.reshape(4, 512, 256), accepted, out_weight, token_embeds, feat_weight, embed_weight,
    )
    draft, new_state = pl.pallas_call(
        finish,
        out_shape=(
            jax.ShapeDtypeStruct((4, 8, 512), bf16),
            jax.ShapeDtypeStruct((4, 512, 256), bf16),
        ),
        in_specs=[hbm] * 2,
        out_specs=(hbm, hbm),
        scratch_shapes=[pltpu.VMEM((4, 8, 512), bf16), pltpu.VMEM((4, 512, 256), bf16), dma((10,))],
        name="results",
    )(draft, new_state)
    return draft, new_state.reshape(4, 8, 64, 256)


def solution(mesh):
    in_specs = (
        P("row", None, "tensor"),
        P("row", None, "tensor"),
        P("row", None, "tensor"),
        P("row", None, "tensor"),
        P("row", None, "tensor"),
        P("tensor"),
        P("tensor"),
        P("tensor"),
        P("tensor"),
        P("row", "tensor", None, None),
        P("row"),
        P("tensor", "row"),
        P("tensor", None, "row"),
        P("row", "tensor"),
        P("row", "tensor"),
    )
    out_specs = (P("row", None, "tensor"), P("row", "tensor", None, None))
    return jax.shard_map(body, mesh=mesh, in_specs=in_specs, out_specs=out_specs, check_vma=False)
```
